32 devices in a mesh: groups: 2 (over x), orient: 8 (over z, y), tile: 2 (over core).
Axes of the slice: x: 2, y: 2, z: 4, core: 2. Of those that a mesh axis runs over, the one named last changes fastest.
Arguments:
- spectra: float32 [16, 2, 256, 256], P(('groups', 'orient'), None, 'tile'), parts along dimension 0, may hold values from -6 to 6
- templates: float32 [8, 2, 256, 256], P('orient', None, 'tile'), may hold values from -1600 to 1600, as said below
- weights: float32 [512, 256], P('groups'), parts along dimension 0, may hold values from 0.1 to 1
Outputs:
- peak: float32 [16, 256, 256], P(('groups', 'orient'), 'tile'), parts along dimension 0
- mean_map: float32 [16, 256, 256], P(('groups', 'orient'), 'tile'), parts along dimension 0
- mean_square: float32 [16, 256, 256], P(('groups', 'orient'), 'tile'), parts along dimension 0
The draws below stay inside these ranges and needn't reach their ends.
There are 2 independent parts, one for each index of `groups`. The reference program is written for one: setup_inputs(seed, part) draws one part's arguments, and reference() takes and returns one part's arrays. A program takes and returns all parts, laid end to end along the dimension named above; an argument that names none is the same for every part. Nothing has to cross between parts.
Inputs may be any that keep to these rules, and one draw needn't show every extreme that they name: `templates`: finite real values.
All inputs are finite; a program needn't handle non-finite values.
Results may differ from the reference program's by a relative error of at most 0.00029.
Values sent between devices are 32-bit elements; how exact they have to be, the bound alone decides.
No kernel may reach another device: no remote copies, remote signals or barrier semaphores. Data moves between devices by JAX's collectives and lax.ppermute only.
A program may use at most 64 MiB of HBM per device.

```python
import math
import jax
import jax.numpy as jnp
from jax import lax

L = 256
TILES = 8
ORIENTS = 8


def draw_templates(key, part):
    base_key = jax.random.fold_in(key, 11)
    row_key = jax.random.fold_in(key, 12)
    col_key = jax.random.fold_in(key, 13)
    shape = (ORIENTS, 2, L, L)
    base = jnp.clip(jax.random.normal(base_key, shape, jnp.float32), -6.0, 6.0)
    row_scale = jnp.exp(jax.random.uniform(row_key, (ORIENTS, 1, L, 1), jnp.float32, 0.0, 2.3))
    col_scale = jnp.exp(jax.random.uniform(col_key, (ORIENTS, 1, 1, L), jnp.float32, 0.0, 2.3))
    return base * row_scale * col_scale


def block_levels(key, extent, shards, smallest, high):
    def one(position, blocks):
        draws = jax.random.uniform(jax.random.fold_in(jax.random.fold_in(key, 6), position), (blocks,), jnp.float32, smallest / len(shards), high / len(shards))
        return jnp.repeat(jnp.exp(draws), extent[position] // blocks).reshape((-1,) + (1,) * (len(extent) - position - 1))

    level = one(*shards[0])
    for cut in shards[1:]:
        level = level * one(*cut)
    return level


def bell_draw(key, shape, deviation, most, split=(), held_as=jnp.bfloat16):
    entries = deviation * jax.random.normal(key, shape, jnp.float32)
    if split:
        entries = entries * block_levels(key, shape, split, -0.22, 0.18)
    return jnp.clip(entries, -most, most).astype(held_as)


def setup_inputs(seed: int = 0, part: int = 0) -> dict:
    streams_of = jax.random.split(jax.random.key(seed), 4)
    own_keys = jax.random.split(jax.random.fold_in(streams_of[3], part), 4)
    spectra = bell_draw(own_keys[0], (TILES, 2, L, L), 1.0, 6.0, ((0, 8), (2, 2)), jnp.float32)
    templates = draw_templates(jax.random.fold_in(streams_of[3], 71), part)
    weights = jnp.clip(jnp.exp(jax.random.uniform(own_keys[2], (L, L), jnp.float32, math.log(0.1), math.log(1.0))), 0.1, 1.0)
    return {"spectra": spectra, "templates": templates, "weights": weights}


def correlate(spectrum, normed_one, weights):
    real_part = (spectrum[0] * normed_one[0] + spectrum[1] * normed_one[1]) * weights
    imag_part = (spectrum[1] * normed_one[0] - spectrum[0] * normed_one[1]) * weights
    side = spectrum.shape[-1]
    return jnp.real(jnp.fft.ifft2(real_part + 1j * imag_part)) * side

def reference(spectra, templates, weights):
    power = lax.optimization_barrier(jnp.mean(templates * templates, axis=(1, 2, 3), keepdims=True))
    normed = templates / jnp.sqrt(power + 1e-06)

    def per_tile(spectrum):
        maps = lax.map(lambda one: correlate(spectrum, one, weights), normed)
        return (lax.optimization_barrier(jnp.max(maps, 0)), lax.optimization_barrier(jnp.mean(maps, 0)), lax.optimization_barrier(jnp.mean(maps * maps, 0)))
    peak, mean_map, mean_square = lax.map(per_tile, spectra)
    return (peak, mean_map, mean_square)
```

```python
import functools
import math

import jax
import jax.numpy as jnp
import numpy as np
from jax import lax
from jax.experimental import pallas as pl
from jax.experimental.pallas import tpu as pltpu
from jax.sharding import PartitionSpec as P


def split_table(table):
    table = table.astype(np.float32)
    high = table.astype(jnp.bfloat16)
    low = (table - high.astype(np.float32)).astype(jnp.bfloat16)
    return np.stack([high, low])


def column_table(side):
    mid = side // 2
    k = np.arange(side)[:, None]
    x = np.arange(mid)[None, :]
    angle = 2.0 * math.pi * (k * x % side) / side
    right = np.sin(angle)
    right[:, 0] = np.cos(math.pi * k[:, 0])
    return split_table(np.concatenate([np.cos(angle), right], 1))


def row_table(side, half):
    y = np.arange(side)[:, None]
    k = np.arange(half)[None, :]
    angle = 2.0 * math.pi * (k * y % side) / side
    return split_table(np.concatenate([np.cos(angle), -np.sin(angle)], 1))


def unfold_table(mid):
    table = np.zeros((mid, mid), np.float32)
    k = np.arange(mid)
    table[(mid - k) % mid, k] = 1.0
    return table


def parts(x):
    high = x.astype(jnp.bfloat16)
    low = (x - high.astype(jnp.float32)).astype(jnp.bfloat16)
    return high, low


def dot(a, b):
    return jnp.dot(a, b, preferred_element_type=jnp.float32)


def correlate_kernel(s_ref, w_ref, q_ref, col_ref, row_ref, keep_ref, send_ref, sw_ref, rt_ref):
    half, side = s_ref.shape[1], s_ref.shape[2]
    mid = side // 2
    here = lax.axis_index("tile")

    @pl.when(pl.program_id(0) == 0)
    def _():
        w = w_ref[pl.ds(pl.multiple_of(here * half, half), half), :]
        sw_ref[0] = s_ref[0] * w
        sw_ref[1] = s_ref[1] * w
        odd = lax.broadcasted_iota(jnp.int32, (half, side), 0) % 2
        sign = (1 - 2 * odd * here).astype(jnp.float32)
        for n in range(2):
            mine = row_ref[n, pl.ds(pl.multiple_of(here * half, half), half), :].astype(jnp.float32)
            other = row_ref[n, pl.ds(pl.multiple_of((1 - here) * half, half), half), :].astype(jnp.float32)
            rt_ref[n, :half] = (mine * sign).astype(jnp.bfloat16)
            rt_ref[n, half:] = (other * sign).astype(jnp.bfloat16)

    sr, si = sw_ref[0], sw_ref[1]
    qr, qi = q_ref[0, 0], q_ref[0, 1]
    squares = jnp.sum((qr * qr + qi * qi).reshape(half // 8, 8, side), axis=0)
    power = jnp.broadcast_to(jnp.sum(squares), (8, side))
    z = jnp.concatenate([sr * qr + si * qi, si * qr - sr * qi], 0)
    zh, zl = parts(z)
    ch, cl = col_ref[0], col_ref[1]
    m = dot(zh, ch) + (dot(zl, ch) + dot(zh, cl))
    mcr, mci = m[:half, :mid], m[half:, :mid]
    msr, msi = m[:half, mid:], m[half:, mid:]
    first = lax.broadcasted_iota(jnp.int32, (half, mid), 1) == 0
    real = jnp.concatenate([mcr - jnp.where(first, 0.0, msi), jnp.where(first, msr, mcr + msi)], 1)
    imag = jnp.concatenate([mci + jnp.where(first, 0.0, msr), jnp.where(first, msi, mci - msr)], 1)
    ah, al = parts(jnp.concatenate([real, imag], 0))
    rh, rl = rt_ref[0], rt_ref[1]
    p = dot(rh, ah) + (dot(rh, al) + dot(rl, ah))
    keep_ref[0, :half] = p[:half]
    keep_ref[0, half:] = power
    send_ref[0, :half] = p[half:]
    send_ref[0, half:] = power


def stats_kernel(count, entries, keep_ref, recv_ref, fold_ref, peak_ref, mean_ref, square_ref, flip_ref):
    side = keep_ref.shape[2]
    half = keep_ref.shape[1] - 8
    mid = side // 2
    for block in range(half // 8):
        rows = pl.ds(block * 8, 8)
        best = total = squares = None
        for o in range(count):
            power = (keep_ref[o, half:] + recv_ref[o, half:]) * (1.0 / entries)
            scale = lax.rsqrt(power + 1e-6) * (1.0 / side)
            c = (keep_ref[o, rows] + recv_ref[o, rows]) * scale
            if o == 0:
                best, total, squares = c, c, c * c
            else:
                best, total, squares = jnp.maximum(best, c), total + c, squares + c * c
        total = total * (1.0 / count)
        squares = squares * (1.0 / count)
        for n, (ref, value) in enumerate(((peak_ref, best), (mean_ref, total), (square_ref, squares))):
            ref[0, rows, :mid] = value[:, :mid]
            flip_ref[pl.ds(n * half + block * 8, 8)] = value[:, mid:]
    right = jnp.dot(flip_ref[...], fold_ref[...], precision=lax.Precision.HIGHEST, preferred_element_type=jnp.float32)
    for n, ref in enumerate((peak_ref, mean_ref, square_ref)):
        ref[0, :, mid:] = right[n * half:(n + 1) * half]


def shards(spectra, templates, weights):
    half, side = spectra.shape[2:]
    gathered = lax.all_gather(templates[0], "orient", axis=0)
    count = gathered.shape[0]
    whole = lambda *shape: pl.BlockSpec(shape, lambda i: (0,) * len(shape))
    one = lambda *shape: pl.BlockSpec((1,) + shape, lambda i: (i,) + (0,) * len(shape))
    keep, send = pl.pallas_call(
        correlate_kernel,
        grid=(count,),
        in_specs=[whole(2, half, side), whole(side, side), one(2, half, side), whole(2, side, side), whole(2, side, side)],
        out_specs=[one(half + 8, side)] * 2,
        out_shape=[jax.ShapeDtypeStruct((count, half + 8, side), jnp.float32)] * 2,
        scratch_shapes=[pltpu.VMEM((2, half, side), jnp.float32), pltpu.VMEM((2, side, side), jnp.bfloat16)],
        compiler_params=pltpu.CompilerParams(vmem_limit_bytes=24 << 20),
        name="correlate",
    )(spectra[0], weights, gathered, jnp.asarray(column_table(side)), jnp.asarray(row_table(side, half)))
    recv = lax.ppermute(send, "tile", [(0, 1), (1, 0)])
    vmem = pl.BlockSpec(memory_space=pltpu.VMEM)
    out = jax.ShapeDtypeStruct((1, half, side), jnp.float32)
    return tuple(pl.pallas_call(
        functools.partial(stats_kernel, count, 2 * side * side),
        in_specs=[vmem] * 3,
        out_specs=[vmem] * 3,
        out_shape=[out] * 3,
        scratch_shapes=[pltpu.VMEM((3 * half, side // 2), jnp.float32)],
        compiler_params=pltpu.CompilerParams(vmem_limit_bytes=24 << 20),
        name="statistics",
    )(keep, recv, jnp.asarray(unfold_table(side // 2))))


def solution(mesh):
    in_specs = (
        P(("groups", "orient"), None, "tile", None),
        P("orient", None, "tile", None),
        P("groups", None),
    )
    out_specs = (P(("groups", "orient"), "tile", None),) * 3
    return jax.shard_map(shards, mesh=mesh, in_specs=in_specs, out_specs=out_specs, check_vma=False)
```

```python
import functools
import math

import jax
import jax.numpy as jnp
import numpy as np
from jax import lax
from jax.experimental import pallas as pl
from jax.experimental.pallas import tpu as pltpu
from jax.sharding import PartitionSpec as P


def split_table(table):
    table = table.astype(np.float32)
    high = table.astype(jnp.bfloat16)
    low = (table - high.astype(np.float32)).astype(jnp.bfloat16)
    return np.stack([high, low])


def column_table(side):
    mid = side // 2
    k = np.arange(side)[:, None]
    x = np.arange(mid)[None, :]
    angle = 2.0 * math.pi * (k * x % side) / side
    right = np.sin(angle)
    right[:, 0] = np.cos(math.pi * k[:, 0])
    return split_table(np.concatenate([np.cos(angle), right], 1))


def row_table(side, half):
    y = np.arange(side)[:, None]
    k = np.arange(half)[None, :]
    angle = 2.0 * math.pi * (k * y % side) / side
    return split_table(np.concatenate([np.cos(angle), -np.sin(angle)], 1))


def unfold_table(mid):
    table = np.zeros((mid, mid), np.float32)
    k = np.arange(mid)
    table[(mid - k) % mid, k] = 1.0
    return table


def parts(x):
    high = x.astype(jnp.bfloat16)
    low = (x - high.astype(jnp.float32)).astype(jnp.bfloat16)
    return high, low


def dot(a, b):
    return jnp.dot(a, b, preferred_element_type=jnp.float32)


def prepare(s_ref, w_ref, row_ref, coef_ref, rt_ref):
    half, side = s_ref.shape[1], s_ref.shape[2]
    here = lax.axis_index("tile")
    swap = lax.axis_index("groups") % 2
    mine = pl.ds(pl.multiple_of(here * half, half), half)
    other = pl.ds(pl.multiple_of((1 - here) * half, half), half)
    w = w_ref[mine, :]
    u, v = s_ref[swap] * w, s_ref[1 - swap] * w
    turn = (1 - 2 * swap).astype(jnp.float32)
    coef_ref[0], coef_ref[1], coef_ref[2], coef_ref[3] = u, v, u * turn, v * turn
    odd = lax.broadcasted_iota(jnp.int32, (half, side), 0) % 2
    sign = (1 - 2 * odd * here).astype(jnp.float32)
    for n in range(2):
        rt_ref[n, :half] = (row_ref[n, mine, :].astype(jnp.float32) * sign).astype(jnp.bfloat16)
        rt_ref[n, half:] = (row_ref[n, other, :].astype(jnp.float32) * sign).astype(jnp.bfloat16)


def correlate(a, b, coef_ref, col_ref, rt_ref, keep_ref, send_ref, n):
    half, side = a.shape
    mid = side // 2
    squares = jnp.sum((a * a + b * b).reshape(half // 8, 8, side), axis=0)
    power = jnp.broadcast_to(jnp.sum(squares), (8, side))
    z = jnp.concatenate([coef_ref[0] * a + coef_ref[1] * b, coef_ref[3] * a - coef_ref[2] * b], 0)
    zh, zl = parts(z)
    ch, cl = col_ref[0], col_ref[1]
    m = dot(zh, ch) + (dot(zl, ch) + dot(zh, cl))
    mcr, mci = m[:half, :mid], m[half:, :mid]
    msr, msi = m[:half, mid:], m[half:, mid:]
    first = lax.broadcasted_iota(jnp.int32, (half, mid), 1) == 0
    real = jnp.concatenate([mcr - jnp.where(first, 0.0, msi), jnp.where(first, msr, mcr + msi)], 1)
    imag = jnp.concatenate([mci + jnp.where(first, 0.0, msr), jnp.where(first, msi, mci - msr)], 1)
    ah, al = parts(jnp.concatenate([real, imag], 0))
    rh, rl = rt_ref[0], rt_ref[1]
    p = dot(rh, ah) + (dot(rh, al) + dot(rl, ah))
    keep_ref[n, :half] = p[:half]
    keep_ref[n, half:] = power
    send_ref[n, :half] = p[half:]
    send_ref[n, half:] = power


def first_kernel(s_ref, w_ref, row_ref, col_ref, t_ref, coef_ref, rt_ref, keep_ref, send_ref):
    prepare(s_ref, w_ref, row_ref, coef_ref, rt_ref)
    swap = lax.axis_index("groups") % 2
    correlate(t_ref[swap], t_ref[1 - swap], coef_ref, col_ref, rt_ref, keep_ref, send_ref, 0)


def more_kernel(wholes, coef_ref, rt_ref, col_ref, *refs):
    inputs, (keep_ref, send_ref) = refs[:-2], refs[-2:]
    swap = lax.axis_index("groups") % 2
    n = 0
    for ref in inputs[:wholes]:
        for i in range(ref.shape[0] // 2):
            correlate(ref[2 * i + swap], ref[2 * i + 1 - swap], coef_ref, col_ref, rt_ref, keep_ref, send_ref, n)
            n += 1
    for a_ref, b_ref in zip(inputs[wholes::2], inputs[wholes + 1::2]):
        correlate(a_ref[...], b_ref[...], coef_ref, col_ref, rt_ref, keep_ref, send_ref, n)
        n += 1


def stats_kernel(calls, entries, *refs):
    keeps, recvs = refs[:calls], refs[calls:2 * calls]
    fold_ref, peak_ref, mean_ref, square_ref, flip_ref = refs[2 * calls:]
    side = keeps[0].shape[2]
    half = keeps[0].shape[1] - 8
    mid = side // 2
    pairs = [(keep, recv, n) for keep, recv in zip(keeps, recvs) for n in range(keep.shape[0])]
    count = len(pairs)
    for block in range(half // 8):
        rows = pl.ds(block * 8, 8)
        best = total = squares = None
        for keep, recv, n in pairs:
            power = (keep[n, half:] + recv[n, half:]) * (1.0 / entries)
            scale = lax.rsqrt(power + 1e-6) * (1.0 / side)
            c = (keep[n, rows] + recv[n, rows]) * scale
            if best is None:
                best, total, squares = c, c, c * c
            else:
                best, total, squares = jnp.maximum(best, c), total + c, squares + c * c
        total = total * (1.0 / count)
        squares = squares * (1.0 / count)
        for n, (ref, value) in enumerate(((peak_ref, best), (mean_ref, total), (square_ref, squares))):
            ref[0, rows, :mid] = value[:, :mid]
            flip_ref[pl.ds(n * half + block * 8, 8)] = value[:, mid:]
    right = jnp.dot(flip_ref[...], fold_ref[...], precision=lax.Precision.HIGHEST, preferred_element_type=jnp.float32)
    for n, ref in enumerate((peak_ref, mean_ref, square_ref)):
        ref[0, :, mid:] = right[n * half:(n + 1) * half]


def flipped(x, axis, bits):
    return lax.ppermute(x, axis, [(i, i ^ bits) for i in range(lax.axis_size(axis))])


def fetch(template):
    orients = lax.axis_size("orient")
    if lax.axis_size("groups") != 2 or orients != 8:
        rest = [flipped(template, "orient", k) for k in range(1, orients)]
        return [(rest[i:i + 2], []) for i in range(0, len(rest), 2)]
    part = lax.dynamic_index_in_dim(template, lax.axis_index("groups"), 0, keepdims=False)
    beside = flipped(template, "orient", 1)
    far = [flipped(part, "orient", 2 * k) for k in (1, 2, 3)]
    sets = []
    for k, mine in enumerate(far):
        partner = flipped(mine, "groups", 1)
        column = flipped(mine, "orient", 1)
        corner = flipped(column, "groups", 1) if k < 2 else flipped(partner, "orient", 1)
        sets.append(([beside] if k == 0 else [], [mine, partner, column, corner]))
    return sets


def shards(spectra, templates, weights):
    half, side = spectra.shape[2:]
    vmem = pl.BlockSpec(memory_space=pltpu.VMEM)
    params = pltpu.CompilerParams(vmem_limit_bytes=24 << 20)
    shape = lambda *dims, dtype=jnp.float32: jax.ShapeDtypeStruct(dims, dtype)
    columns = jnp.asarray(column_table(side))
    rows = jnp.asarray(row_table(side, half))
    coef, table, keep, send = pl.pallas_call(
        first_kernel,
        in_specs=[vmem] * 5,
        out_specs=[vmem] * 4,
        out_shape=[shape(4, half, side), shape(2, side, side, dtype=jnp.bfloat16)] + [shape(1, half + 8, side)] * 2,
        compiler_params=params,
        name="first",
    )(spectra[0], weights, rows, columns, templates[0])
    keeps, recvs = [keep], [flipped(send, "tile", 1)]
    for wholes, pieces in fetch(templates[0]):
        count = len(wholes) + len(pieces) // 2
        keep, send = pl.pallas_call(
            functools.partial(more_kernel, len(wholes)),
            in_specs=[vmem] * (3 + len(wholes) + len(pieces)),
            out_specs=[vmem] * 2,
            out_shape=[shape(count, half + 8, side)] * 2,
            compiler_params=params,
            name="more",
        )(coef, table, columns, *wholes, *pieces)
        keeps.append(keep)
        recvs.append(flipped(send, "tile", 1))
    return tuple(pl.pallas_call(
        functools.partial(stats_kernel, len(keeps), 2 * side * side),
        in_specs=[vmem] * (2 * len(keeps) + 1),
        out_specs=[vmem] * 3,
        out_shape=[shape(1, half, side)] * 3,
        scratch_shapes=[pltpu.VMEM((3 * half, side // 2), jnp.float32)],
        compiler_params=params,
        name="statistics",
    )(*keeps, *recvs, jnp.asarray(unfold_table(side // 2))))


def solution(mesh):
    in_specs = (
        P(("groups", "orient"), None, "tile", None),
        P("orient", None, "tile", None),
        P("groups", None),
    )
    out_specs = (P(("groups", "orient"), "tile", None),) * 3
    return jax.shard_map(shards, mesh=mesh, in_specs=in_specs, out_specs=out_specs, check_vma=False)
```

```python
import functools
import math

import jax
import jax.numpy as jnp
import numpy as np
from jax import lax
from jax.experimental import pallas as pl
from jax.experimental.pallas import tpu as pltpu
from jax.sharding import PartitionSpec as P


def split_table(table):
    table = table.astype(np.float32)
    high = table.astype(jnp.bfloat16)
    low = (table - high.astype(np.float32)).astype(jnp.bfloat16)
    return np.stack([high, low])


def column_table(side):
    mid = side // 2
    k = np.arange(side)[:, None]
    x = np.arange(mid)[None, :]
    angle = 2.0 * math.pi * (k * x % side) / side
    right = np.sin(angle)
    right[:, 0] = np.cos(math.pi * k[:, 0])
    return split_table(np.concatenate([np.cos(angle), right], 1))


def row_table(side, half):
    y = np.arange(side)[:, None]
    k = np.arange(half)[None, :]
    angle = 2.0 * math.pi * (k * y % side) / side
    return split_table(np.concatenate([np.cos(angle), -np.sin(angle)], 1))


def unfold_table(mid):
    table = np.zeros((mid, mid), np.float32)
    k = np.arange(mid)
    table[(mid - k) % mid, k] = 1.0
    return table


def parts(x):
    high = x.astype(jnp.bfloat16)
    low = (x - high.astype(jnp.float32)).astype(jnp.bfloat16)
    return high, low


def dot(a, b):
    return jnp.dot(a, b, preferred_element_type=jnp.float32)


def prepare(s_ref, w_ref, row_ref, coef_ref, rt_ref):
    half, side = s_ref.shape[1], s_ref.shape[2]
    here = lax.axis_index("tile")
    swap = lax.axis_index("groups") % 2
    mine = pl.ds(pl.multiple_of(here * half, half), half)
    other = pl.ds(pl.multiple_of((1 - here) * half, half), half)
    w = w_ref[mine, :]
    u, v = s_ref[swap] * w, s_ref[1 - swap] * w
    turn = (1 - 2 * swap).astype(jnp.float32)
    coef_ref[0], coef_ref[1], coef_ref[2], coef_ref[3] = u, v, u * turn, v * turn
    odd = lax.broadcasted_iota(jnp.int32, (half, side), 0) % 2
    sign = (1 - 2 * odd * here).astype(jnp.float32)
    for n in range(2):
        rt_ref[n, :half] = (row_ref[n, mine, :].astype(jnp.float32) * sign).astype(jnp.bfloat16)
        rt_ref[n, half:] = (row_ref[n, other, :].astype(jnp.float32) * sign).astype(jnp.bfloat16)


def correlate(a, b, coef_ref, col_ref, rt_ref, keep_ref, send_ref, n):
    half, side = a.shape
    mid = side // 2
    squares = jnp.sum((a * a + b * b).reshape(half // 8, 8, side), axis=0)
    power = jnp.broadcast_to(jnp.sum(squares), (8, side))
    z = jnp.concatenate([coef_ref[0] * a + coef_ref[1] * b, coef_ref[3] * a - coef_ref[2] * b], 0)
    zh, zl = parts(z)
    ch, cl = col_ref[0], col_ref[1]
    m = dot(zh, ch) + (dot(zl, ch) + dot(zh, cl))
    mcr, mci = m[:half, :mid], m[half:, :mid]
    msr, msi = m[:half, mid:], m[half:, mid:]
    first = lax.broadcasted_iota(jnp.int32, (half, mid), 1) == 0
    real = jnp.concatenate([mcr - jnp.where(first, 0.0, msi), jnp.where(first, msr, mcr + msi)], 1)
    imag = jnp.concatenate([mci + jnp.where(first, 0.0, msr), jnp.where(first, msi, mci - msr)], 1)
    ah, al = parts(jnp.concatenate([real, imag], 0))
    rh, rl = rt_ref[0], rt_ref[1]
    p = dot(rh, ah) + (dot(rh, al) + dot(rl, ah))
    keep_ref[n, :half] = p[:half]
    keep_ref[n, half:] = power
    send_ref[n, :half] = p[half:]
    send_ref[n, half:] = power


def first_kernel(s_ref, w_ref, row_ref, col_ref, t_ref, coef_ref, rt_ref, keep_ref, send_ref):
    prepare(s_ref, w_ref, row_ref, coef_ref, rt_ref)
    swap = lax.axis_index("groups") % 2
    correlate(t_ref[swap], t_ref[1 - swap], coef_ref, col_ref, rt_ref, keep_ref, send_ref, 0)


def more_kernel(wholes, places, coef_ref, rt_ref, col_ref, *refs):
    inputs, (keep_ref, send_ref) = refs[:-2], refs[-2:]
    whole_refs, part_refs = inputs[:wholes], inputs[wholes:]
    swap = lax.axis_index("groups") % 2
    for n, ref in enumerate(whole_refs):
        correlate(ref[swap], ref[1 - swap], coef_ref, col_ref, rt_ref, keep_ref, send_ref, n)
    for i in range(0, len(places), 2):
        a, b = (part_refs[array][index] for array, index in places[i:i + 2])
        correlate(a, b, coef_ref, col_ref, rt_ref, keep_ref, send_ref, wholes + i // 2)


def stats_kernel(calls, entries, *refs):
    keeps, recvs = refs[:calls], refs[calls:2 * calls]
    fold_ref, peak_ref, mean_ref, square_ref, flip_ref = refs[2 * calls:]
    side = keeps[0].shape[2]
    half = keeps[0].shape[1] - 8
    mid = side // 2
    pairs = [(keep, recv, n) for keep, recv in zip(keeps, recvs) for n in range(keep.shape[0])]
    count = len(pairs)
    for block in range(half // 8):
        rows = pl.ds(block * 8, 8)
        best = total = squares = None
        for keep, recv, n in pairs:
            power = (keep[n, half:] + recv[n, half:]) * (1.0 / entries)
            scale = lax.rsqrt(power + 1e-6) * (1.0 / side)
            c = (keep[n, rows] + recv[n, rows]) * scale
            if best is None:
                best, total, squares = c, c, c * c
            else:
                best, total, squares = jnp.maximum(best, c), total + c, squares + c * c
        total = total * (1.0 / count)
        squares = squares * (1.0 / count)
        for n, (ref, value) in enumerate(((peak_ref, best), (mean_ref, total), (square_ref, squares))):
            ref[0, rows, :mid] = value[:, :mid]
            flip_ref[pl.ds(n * half + block * 8, 8)] = value[:, mid:]
    right = jnp.dot(flip_ref[...], fold_ref[...], precision=lax.Precision.HIGHEST, preferred_element_type=jnp.float32)
    for n, ref in enumerate((peak_ref, mean_ref, square_ref)):
        ref[0, :, mid:] = right[n * half:(n + 1) * half]


def flipped(x, axis, bits):
    return lax.ppermute(x, axis, [(i, i ^ bits) for i in range(lax.axis_size(axis))])


def shards(spectra, templates, weights):
    half, side = spectra.shape[2:]
    orients = lax.axis_size("orient")
    vmem = pl.BlockSpec(memory_space=pltpu.VMEM)
    params = pltpu.CompilerParams(vmem_limit_bytes=24 << 20)
    shape = lambda *dims, dtype=jnp.float32: jax.ShapeDtypeStruct(dims, dtype)
    columns = jnp.asarray(column_table(side))
    rows = jnp.asarray(row_table(side, half))
    template = templates[0]

    def first(template):
        return pl.pallas_call(
            first_kernel,
            in_specs=[vmem] * 5,
            out_specs=[vmem] * 4,
            out_shape=[shape(4, half, side), shape(2, side, side, dtype=jnp.bfloat16)] + [shape(1, half + 8, side)] * 2,
            compiler_params=params,
            name="first",
        )(spectra[0], weights, rows, columns, template)

    def more(coef, table, wholes, *pieces):
        count = len(wholes) + len(pieces) // 2
        arrays = []
        for array, _ in pieces:
            if not any(array is other for other in arrays):
                arrays.append(array)
        places = tuple(([array is other for other in arrays].index(True), index) for array, index in pieces)
        return pl.pallas_call(
            functools.partial(more_kernel, len(wholes), places),
            in_specs=[vmem] * (3 + len(wholes) + len(arrays)),
            out_specs=[vmem] * 2,
            out_shape=[shape(count, half + 8, side)] * 2,
            compiler_params=params,
            name="more",
        )(coef, table, columns, *wholes, *arrays)

    keeps, recvs = [], []

    def swap(keep, send):
        keeps.append(keep)
        recvs.append(flipped(send, "tile", 1))

    if lax.axis_size("groups") == 2 and orients == 8:
        part = lax.dynamic_index_in_dim(template, lax.axis_index("groups"), 0)
        near = [flipped(part, "orient", 2 * k) for k in (1, 2)]
        beside = flipped(template, "orient", 1)
        coef, table, keep, send = first(template)
        near1, near2, late_part, send, beside = lax.optimization_barrier((*near, part, send, beside))
        both = jnp.concatenate([near1, near2], 0)
        far = flipped(late_part, "orient", 6)
        both_x = flipped(both, "groups", 1)
        both_y = flipped(both, "orient", 1)
        swap(keep, send)
        keep, send = more(coef, table, [beside])
        far, both_x, both_y, send = lax.optimization_barrier((far, both_x, both_y, send))
        last_x = flipped(jnp.concatenate([far, both_y[:1]], 0), "groups", 1)
        last_y = flipped(jnp.concatenate([far, both_x[1:]], 0), "orient", 1)
        swap(keep, send)
        keep, send = more(coef, table, [], (both, 0), (both_x, 0), (both, 1), (both_x, 1))
        last_x, last_y, send = lax.optimization_barrier((last_x, last_y, send))
        cut = half // 2
        corner_x = flipped(last_y[:1, :cut], "groups", 1)
        corner_y = flipped(last_x[:1, cut:], "orient", 1)
        swap(keep, send)
        swap(*more(coef, table, [], (both_y, 0), (last_x, 1), (both_y, 1), (last_y, 1), (far, 0), (last_x, 0)))
        corner = jnp.concatenate([corner_x, corner_y], 1)
        swap(*more(coef, table, [], (last_y, 0), (corner, 0)))
    else:
        coef, table, keep, send = first(template)
        swap(keep, send)
        rest = [flipped(template, "orient", k) for k in range(1, orients)]
        for i in range(0, len(rest), 2):
            swap(*more(coef, table, rest[i:i + 2]))
    return tuple(pl.pallas_call(
        functools.partial(stats_kernel, len(keeps), 2 * side * side),
        in_specs=[vmem] * (2 * len(keeps) + 1),
        out_specs=[vmem] * 3,
        out_shape=[shape(1, half, side)] * 3,
        scratch_shapes=[pltpu.VMEM((3 * half, side // 2), jnp.float32)],
        compiler_params=params,
        name="statistics",
    )(*keeps, *recvs, jnp.asarray(unfold_table(side // 2))))


def solution(mesh):
    in_specs = (
        P(("groups", "orient"), None, "tile", None),
        P("orient", None, "tile", None),
        P("groups", None),
    )
    out_specs = (P(("groups", "orient"), "tile", None),) * 3
    return jax.shard_map(shards, mesh=mesh, in_specs=in_specs, out_specs=out_specs, check_vma=False)
```

```python
import functools
import math

import jax
import jax.numpy as jnp
import numpy as np
from jax import lax
from jax.experimental import pallas as pl
from jax.experimental.pallas import tpu as pltpu
from jax.sharding import PartitionSpec as P


def column_table(side):
    mid = side // 2
    k = np.arange(side)[:, None]
    x = np.arange(mid)[None, :]
    angle = 2.0 * math.pi * (k * x % side) / side
    right = np.sin(angle)
    right[:, 0] = np.cos(math.pi * k[:, 0])
    return np.concatenate([np.cos(angle), right], 1).astype(np.float32)


def row_table(side, half):
    y = np.arange(side)[:, None]
    k = np.arange(half)[None, :]
    angle = 2.0 * math.pi * (k * y % side) / side
    return np.concatenate([np.cos(angle), -np.sin(angle)], 1).astype(np.float32)


def unfold_table(mid):
    table = np.zeros((mid, mid), np.float32)
    k = np.arange(mid)
    table[(mid - k) % mid, k] = 1.0
    return table


def parts(x):
    high = x.astype(jnp.bfloat16)
    low = (x - high.astype(jnp.float32)).astype(jnp.bfloat16)
    return high, low


def dot(a, b):
    return jnp.dot(a, b, preferred_element_type=jnp.float32)


def prepare_kernel(s_hbm, w_hbm, row_hbm, col_hbm, coef_ref, rt_ref, ct_ref, s_ref, w_ref, row_ref, col_ref, sems):
    half, side = w_ref.shape
    here = lax.axis_index("tile")
    swap = lax.axis_index("groups") % 2
    mine = pl.ds(pl.multiple_of(here * half, half), half)
    other = pl.ds(pl.multiple_of((1 - here) * half, half), half)
    moves = (
        (s_hbm, s_ref),
        (w_hbm.at[mine], w_ref),
        (row_hbm.at[mine], row_ref.at[pl.ds(0, half)]),
        (row_hbm.at[other], row_ref.at[pl.ds(half, half)]),
        (col_hbm, col_ref),
    )
    copies = [pltpu.make_async_copy(source, target, sems.at[n]) for n, (source, target) in enumerate(moves)]
    for copy in copies:
        copy.start()
    for copy in copies:
        copy.wait()
    w = w_ref[...]
    u, v = s_ref[swap] * w, s_ref[1 - swap] * w
    turn = (1 - 2 * swap).astype(jnp.float32)
    coef_ref[0], coef_ref[1], coef_ref[2], coef_ref[3] = u, v, u * turn, v * turn
    ct_ref[0], ct_ref[1] = parts(col_ref[...])
    odd = lax.broadcasted_iota(jnp.int32, (side, side), 0) % 2
    rt_ref[0], rt_ref[1] = parts(row_ref[...] * (1 - 2 * odd * here).astype(jnp.float32))


def correlate(a, b, coef_ref, col_ref, rt_ref, keep_ref, send_ref, n):
    half, side = a.shape
    mid = side // 2
    squares = jnp.sum((a * a + b * b).reshape(half // 8, 8, side), axis=0)
    power = jnp.broadcast_to(jnp.sum(squares), (8, side))
    z = jnp.concatenate([coef_ref[0] * a + coef_ref[1] * b, coef_ref[3] * a - coef_ref[2] * b], 0)
    zh, zl = parts(z)
    ch, cl = col_ref[0], col_ref[1]
    m = dot(zh, ch) + (dot(zl, ch) + dot(zh, cl))
    mcr, mci = m[:half, :mid], m[half:, :mid]
    msr, msi = m[:half, mid:], m[half:, mid:]
    first = lax.broadcasted_iota(jnp.int32, (half, mid), 1) == 0
    real = jnp.concatenate([mcr - jnp.where(first, 0.0, msi), jnp.where(first, msr, mcr + msi)], 1)
    imag = jnp.concatenate([mci + jnp.where(first, 0.0, msr), jnp.where(first, msi, mci - msr)], 1)
    ah, al = parts(jnp.concatenate([real, imag], 0))
    rh, rl = rt_ref[0], rt_ref[1]
    p = dot(rh, ah) + (dot(rh, al) + dot(rl, ah))
    keep_ref[n, :half] = p[:half]
    keep_ref[n, half:] = power
    send_ref[n, :half] = p[half:]
    send_ref[n, half:] = power


def maps_kernel(wholes, places, coef_ref, rt_ref, col_ref, *refs):
    inputs, (keep_ref, send_ref) = refs[:-2], refs[-2:]
    whole_refs, part_refs = inputs[:wholes], inputs[wholes:]
    swap = lax.axis_index("groups") % 2
    for n, ref in enumerate(whole_refs):
        correlate(ref[swap], ref[1 - swap], coef_ref, col_ref, rt_ref, keep_ref, send_ref, n)
    for n, pair in enumerate(places):
        a, b = (jnp.concatenate([part_refs[array][start:stop] for array, start, stop in piece], 0) for piece in pair)
        correlate(a, b, coef_ref, col_ref, rt_ref, keep_ref, send_ref, wholes + n)


def stats_kernel(calls, entries, *refs):
    keeps, recvs = refs[:calls], refs[calls:2 * calls]
    fold_ref, peak_ref, mean_ref, square_ref, flip_ref = refs[2 * calls:]
    side = keeps[0].shape[2]
    half = keeps[0].shape[1] - 8
    mid = side // 2
    pairs = [(keep, recv, n) for keep, recv in zip(keeps, recvs) for n in range(keep.shape[0])]
    count = len(pairs)
    for block in range(half // 8):
        rows = pl.ds(block * 8, 8)
        best = total = squares = None
        for keep, recv, n in pairs:
            power = (keep[n, half:] + recv[n, half:]) * (1.0 / entries)
            scale = lax.rsqrt(power + 1e-6) * (1.0 / side)
            c = (keep[n, rows] + recv[n, rows]) * scale
            if best is None:
                best, total, squares = c, c, c * c
            else:
                best, total, squares = jnp.maximum(best, c), total + c, squares + c * c
        total = total * (1.0 / count)
        squares = squares * (1.0 / count)
        for n, (ref, value) in enumerate(((peak_ref, best), (mean_ref, total), (square_ref, squares))):
            ref[0, rows, :mid] = value[:, :mid]
            flip_ref[pl.ds(n * half + block * 8, 8)] = value[:, mid:]
    right = jnp.dot(flip_ref[...], fold_ref[...], precision=lax.Precision.HIGHEST, preferred_element_type=jnp.float32)
    for n, ref in enumerate((peak_ref, mean_ref, square_ref)):
        ref[0, :, mid:] = right[n * half:(n + 1) * half]


def flipped(x, axis, bits):
    return lax.ppermute(x, axis, [(i, i ^ bits) for i in range(lax.axis_size(axis))])


def shards(spectra, templates, weights):
    half, side = spectra.shape[2:]
    orients = lax.axis_size("orient")
    vmem = pl.BlockSpec(memory_space=pltpu.VMEM)
    hbm = pl.BlockSpec(memory_space=pltpu.HBM)
    params = pltpu.CompilerParams(vmem_limit_bytes=24 << 20)
    shape = lambda *dims, dtype=jnp.float32: jax.ShapeDtypeStruct(dims, dtype)
    scratch = lambda *dims: pltpu.VMEM(dims, jnp.float32)
    template = templates[0]

    coef, table, columns = pl.pallas_call(
        prepare_kernel,
        in_specs=[hbm] * 4,
        out_specs=[vmem] * 3,
        out_shape=[shape(4, half, side)] + [shape(2, side, side, dtype=jnp.bfloat16)] * 2,
        scratch_shapes=[
            scratch(2, half, side), scratch(half, side), scratch(side, side), scratch(side, side), pltpu.SemaphoreType.DMA((5,)),
        ],
        compiler_params=params,
        name="prepare",
    )(spectra[0], weights, jnp.asarray(row_table(side, half)), jnp.asarray(column_table(side)))

    def maps(wholes, arrays=(), places=()):
        return pl.pallas_call(
            functools.partial(maps_kernel, len(wholes), places),
            in_specs=[vmem] * (3 + len(wholes) + len(arrays)),
            out_specs=[vmem] * 2,
            out_shape=[shape(len(wholes) + len(places), half + 8, side)] * 2,
            compiler_params=params,
            name="maps",
        )(coef, table, columns, *wholes, *arrays)

    if lax.axis_size("groups") == 2 and orients == 8:
        plane = lax.axis_index("groups")
        cut = half // 2
        part = lax.dynamic_index_in_dim(template, plane, 0, keepdims=False)
        near1, near2 = (flipped(part, "orient", 2 * k) for k in (1, 2))
        beside = flipped(template, "orient", 1)
        near1, near2, beside, part, coef = lax.optimization_barrier((near1, near2, beside, part, coef))
        near = jnp.concatenate([near1, near2], 0)
        far = flipped(part, "orient", 6)
        near_x = flipped(near, "groups", 1)
        near_y = flipped(near, "orient", 1)
        rest = lax.dynamic_index_in_dim(template, 1 - plane, 0, keepdims=False)
        far, near_x, near_y, rest = lax.optimization_barrier((far, near_x, near_y, rest))
        last_x = flipped(jnp.concatenate([far, near_y[:half + cut]], 0), "groups", 1)
        last_y = flipped(jnp.concatenate([far, near_x[half + cut:]], 0), "orient", 1)
        corner = flipped(rest, "orient", 7)
        early = maps(
            [template, beside],
            [near, near_x],
            (
                (((0, 0, half),), ((1, 0, half),)),
                (((0, half, side),), ((1, half, side),)),
            ),
        )
        early_recv = flipped(early[1], "tile", 1)
        last_x, last_y, corner, early_recv = lax.optimization_barrier((last_x, last_y, corner, early_recv))
        late = maps(
            [],
            [near_y, last_x, last_y, far, corner],
            (
                (((0, 0, half),), ((1, half, side),)),
                (((0, half, side),), ((1, side, side + cut), (2, half, half + cut))),
                (((3, 0, half),), ((1, 0, half),)),
                (((2, 0, half),), ((4, 0, half),)),
            ),
        )
        keeps, recvs = [early[0], late[0]], [early_recv, flipped(late[1], "tile", 1)]
    else:
        rest = [template] + [flipped(template, "orient", k) for k in range(1, orients)]
        calls = [maps(rest[i:i + 4]) for i in range(0, len(rest), 4)]
        keeps = [keep for keep, _ in calls]
        recvs = [flipped(send, "tile", 1) for _, send in calls]
    return tuple(pl.pallas_call(
        functools.partial(stats_kernel, len(keeps), 2 * side * side),
        in_specs=[vmem] * (2 * len(keeps) + 1),
        out_specs=[vmem] * 3,
        out_shape=[shape(1, half, side)] * 3,
        scratch_shapes=[scratch(3 * half, side // 2)],
        compiler_params=params,
        name="statistics",
    )(*keeps, *recvs, jnp.asarray(unfold_table(side // 2))))


def solution(mesh):
    in_specs = (
        P(("groups", "orient"), None, "tile", None),
        P("orient", None, "tile", None),
        P("groups", None),
    )
    out_specs = (P(("groups", "orient"), "tile", None),) * 3
    return jax.shard_map(shards, mesh=mesh, in_specs=in_specs, out_specs=out_specs, check_vma=False)
```

```python
import functools
import math

import jax
import jax.numpy as jnp
import numpy as np
from jax import lax
from jax.experimental import pallas as pl
from jax.experimental.pallas import tpu as pltpu
from jax.sharding import PartitionSpec as P


def column_table(side):
    mid = side // 2
    k = np.arange(side)[:, None]
    x = np.arange(mid)[None, :]
    angle = 2.0 * math.pi * (k * x % side) / side
    right = np.sin(angle)
    right[:, 0] = np.cos(math.pi * k[:, 0])
    return np.concatenate([np.cos(angle), right], 1).astype(np.float32)


def row_table(side, half):
    y = np.arange(side)[:, None]
    k = np.arange(half)[None, :]
    angle = 2.0 * math.pi * (k * y % side) / side
    return np.concatenate([np.cos(angle), -np.sin(angle)], 1).astype(np.float32)


def unfold_table(mid):
    table = np.zeros((mid, mid), np.float32)
    k = np.arange(mid)
    table[(mid - k) % mid, k] = 1.0
    return table


def parts(x):
    high = x.astype(jnp.bfloat16)
    low = (x - high.astype(jnp.float32)).astype(jnp.bfloat16)
    return high, low


def dot(a, b):
    return jnp.dot(a, b, preferred_element_type=jnp.float32)


def prepare_kernel(s_hbm, w_hbm, row_hbm, col_hbm, coef_ref, rt_ref, ct_ref, s_ref, w_ref, row_ref, col_ref, sems):
    half, side = w_ref.shape
    here = lax.axis_index("tile")
    swap = lax.axis_index("groups") % 2
    mine = pl.ds(pl.multiple_of(here * half, half), half)
    other = pl.ds(pl.multiple_of((1 - here) * half, half), half)
    moves = (
        (s_hbm, s_ref),
        (w_hbm.at[mine], w_ref),
        (row_hbm.at[mine], row_ref.at[pl.ds(0, half)]),
        (row_hbm.at[other], row_ref.at[pl.ds(half, half)]),
        (col_hbm, col_ref),
    )
    copies = [pltpu.make_async_copy(source, target, sems.at[n]) for n, (source, target) in enumerate(moves)]
    for copy in copies:
        copy.start()
    for copy in copies:
        copy.wait()
    w = w_ref[...]
    u, v = s_ref[swap] * w, s_ref[1 - swap] * w
    turn = (1 - 2 * swap).astype(jnp.float32)
    coef_ref[0], coef_ref[1], coef_ref[2], coef_ref[3] = u, v, u * turn, v * turn
    ct_ref[0], ct_ref[1] = parts(col_ref[...])
    odd = lax.broadcasted_iota(jnp.int32, (side, side), 0) % 2
    rt_ref[0], rt_ref[1] = parts(row_ref[...] * (1 - 2 * odd * here).astype(jnp.float32))


def correlate(a, b, coef_ref, col_ref, rt_ref, keep_ref, send_ref, n):
    half, side = a.shape
    mid = side // 2
    squares = jnp.sum((a * a + b * b).reshape(half // 8, 8, side), axis=0)
    power = jnp.broadcast_to(jnp.sum(squares), (keep_ref.shape[1] - half, side))
    z = jnp.concatenate([coef_ref[0] * a + coef_ref[1] * b, coef_ref[3] * a - coef_ref[2] * b], 0)
    zh, zl = parts(z)
    ch, cl = col_ref[0], col_ref[1]
    m = dot(zh, ch) + (dot(zl, ch) + dot(zh, cl))
    mcr, mci = m[:half, :mid], m[half:, :mid]
    msr, msi = m[:half, mid:], m[half:, mid:]
    first = lax.broadcasted_iota(jnp.int32, (half, mid), 1) == 0
    real = jnp.concatenate([mcr - jnp.where(first, 0.0, msi), jnp.where(first, msr, mcr + msi)], 1)
    imag = jnp.concatenate([mci + jnp.where(first, 0.0, msr), jnp.where(first, msi, mci - msr)], 1)
    ah, al = parts(jnp.concatenate([real, imag], 0))
    rh, rl = rt_ref[0], rt_ref[1]
    p = dot(rh, ah) + (dot(rh, al) + dot(rl, ah))
    keep_ref[n, :half] = p[:half]
    keep_ref[n, half:] = power
    send_ref[n, :half] = p[half:]
    send_ref[n, half:] = power


def maps_kernel(wholes, places, coef_ref, rt_ref, col_ref, *refs):
    inputs, (keep_ref, send_ref) = refs[:-2], refs[-2:]
    whole_refs, part_refs = inputs[:wholes], inputs[wholes:]
    swap = lax.axis_index("groups") % 2
    for n, ref in enumerate(whole_refs):
        correlate(ref[swap], ref[1 - swap], coef_ref, col_ref, rt_ref, keep_ref, send_ref, n)
    for n, pair in enumerate(places):
        a, b = (jnp.concatenate([part_refs[array][start:stop] for array, start, stop in piece], 0) for piece in pair)
        correlate(a, b, coef_ref, col_ref, rt_ref, keep_ref, send_ref, wholes + n)


def stats_kernel(calls, entries, *refs):
    keeps, recvs = refs[:calls], refs[calls:2 * calls]
    fold_ref, peak_ref, mean_ref, square_ref, flip_ref = refs[2 * calls:]
    half, side = peak_ref.shape[1:]
    mid = side // 2
    pairs = [(keep, recv, n) for keep, recv in zip(keeps, recvs) for n in range(keep.shape[0])]
    count = len(pairs)
    for block in range(half // 8):
        rows = pl.ds(block * 8, 8)
        best = total = squares = None
        for keep, recv, n in pairs:
            power = (keep[n, half:half + 8] + recv[n, half:half + 8]) * (1.0 / entries)
            scale = lax.rsqrt(power + 1e-6) * (1.0 / side)
            c = (keep[n, rows] + recv[n, rows]) * scale
            if best is None:
                best, total, squares = c, c, c * c
            else:
                best, total, squares = jnp.maximum(best, c), total + c, squares + c * c
        total = total * (1.0 / count)
        squares = squares * (1.0 / count)
        for n, (ref, value) in enumerate(((peak_ref, best), (mean_ref, total), (square_ref, squares))):
            ref[0, rows, :mid] = value[:, :mid]
            flip_ref[pl.ds(n * half + block * 8, 8)] = value[:, mid:]
    right = jnp.dot(flip_ref[...], fold_ref[...], precision=lax.Precision.HIGHEST, preferred_element_type=jnp.float32)
    for n, ref in enumerate((peak_ref, mean_ref, square_ref)):
        ref[0, :, mid:] = right[n * half:(n + 1) * half]


def flipped(x, axis, bits):
    return lax.ppermute(x, axis, [(i, i ^ bits) for i in range(lax.axis_size(axis))])


def shards(spectra, templates, weights):
    half, side = spectra.shape[2:]
    orients = lax.axis_size("orient")
    vmem = pl.BlockSpec(memory_space=pltpu.VMEM)
    hbm = pl.BlockSpec(memory_space=pltpu.HBM)
    params = pltpu.CompilerParams(vmem_limit_bytes=24 << 20)
    shape = lambda *dims, dtype=jnp.float32: jax.ShapeDtypeStruct(dims, dtype)
    scratch = lambda *dims: pltpu.VMEM(dims, jnp.float32)
    template = templates[0]

    coef, table, columns = pl.pallas_call(
        prepare_kernel,
        in_specs=[hbm] * 4,
        out_specs=[vmem] * 3,
        out_shape=[shape(4, half, side)] + [shape(2, side, side, dtype=jnp.bfloat16)] * 2,
        scratch_shapes=[
            scratch(2, half, side), scratch(half, side), scratch(side, side), scratch(side, side), pltpu.SemaphoreType.DMA((5,)),
        ],
        compiler_params=params,
        name="prepare",
    )(spectra[0], weights, jnp.asarray(row_table(side, half)), jnp.asarray(column_table(side)))

    def maps(wholes, arrays=(), places=(), extra=8):
        return pl.pallas_call(
            functools.partial(maps_kernel, len(wholes), places),
            in_specs=[vmem] * (3 + len(wholes) + len(arrays)),
            out_specs=[vmem] * 2,
            out_shape=[shape(len(wholes) + len(places), half + extra, side)] * 2,
            compiler_params=params,
            name="maps",
        )(coef, table, columns, *wholes, *arrays)

    if lax.axis_size("groups") == 2 and orients == 8:
        cut = half // 2
        part = lax.dynamic_index_in_dim(template, lax.axis_index("groups"), 0, keepdims=False)
        near1, near2 = (flipped(part, "orient", 2 * k) for k in (1, 2))
        beside = flipped(lax.optimization_barrier((template, part))[0], "orient", 1)
        near1, near2, beside, coef = lax.optimization_barrier((near1, near2, beside, coef))
        near = jnp.concatenate([near1, near2], 0)
        far = flipped(near2, "orient", 2)
        near_x = flipped(near, "groups", 1)
        near_y = flipped(near, "orient", 1)
        far, near_x, near_y = lax.optimization_barrier((far, near_x, near_y))
        last_x = flipped(jnp.concatenate([far, near_y[:half + cut]], 0), "groups", 1)
        last_y = flipped(jnp.concatenate([far, near_x[half + cut:]], 0), "orient", 1)
        corner = flipped(near_x[half:], "orient", 3)
        early = maps(
            [template, beside],
            [near, near_x],
            (
                (((0, 0, half),), ((1, 0, half),)),
                (((0, half, side),), ((1, half, side),)),
            ),
            16,
        )
        last_x, last_y, corner, early = lax.optimization_barrier((last_x, last_y, corner, early))
        late = maps(
            [],
            [near_y, last_x, last_y, far, corner],
            (
                (((0, 0, half),), ((1, half, side),)),
                (((0, half, side),), ((1, side, side + cut), (2, half, half + cut))),
                (((3, 0, half),), ((1, 0, half),)),
                (((2, 0, half),), ((4, 0, half),)),
            ),
        )
        calls = [early, late]
    else:
        rest = [template] + [flipped(template, "orient", k) for k in range(1, orients)]
        calls = [maps(rest[i:i + 4]) for i in range(0, len(rest), 4)]
    keeps = [keep for keep, _ in calls]
    recvs = [flipped(send, "tile", 1) for _, send in calls]
    return tuple(pl.pallas_call(
        functools.partial(stats_kernel, len(keeps), 2 * side * side),
        in_specs=[vmem] * (2 * len(keeps) + 1),
        out_specs=[vmem] * 3,
        out_shape=[shape(1, half, side)] * 3,
        scratch_shapes=[scratch(3 * half, side // 2)],
        compiler_params=params,
        name="statistics",
    )(*keeps, *recvs, jnp.asarray(unfold_table(side // 2))))


def solution(mesh):
    in_specs = (
        P(("groups", "orient"), None, "tile", None),
        P("orient", None, "tile", None),
        P("groups", None),
    )
    out_specs = (P(("groups", "orient"), "tile", None),) * 3
    return jax.shard_map(shards, mesh=mesh, in_specs=in_specs, out_specs=out_specs, check_vma=False)
```

```python
import functools
import math

import jax
import jax.numpy as jnp
import numpy as np
from jax import lax
from jax.experimental import pallas as pl
from jax.experimental.pallas import tpu as pltpu
from jax.sharding import PartitionSpec as P


def column_table(side):
    mid = side // 2
    k = np.arange(side)[:, None]
    x = np.arange(mid)[None, :]
    angle = 2.0 * math.pi * (k * x % side) / side
    right = np.sin(angle)
    right[:, 0] = np.cos(math.pi * k[:, 0])
    return np.concatenate([np.cos(angle), right], 1).astype(np.float32)


def row_table(side, half):
    y = np.arange(side)[:, None]
    k = np.arange(half)[None, :]
    angle = 2.0 * math.pi * (k * y % side) / side
    return np.concatenate([np.cos(angle), -np.sin(angle)], 1).astype(np.float32)


def unfold_table(mid):
    table = np.zeros((mid, mid), np.float32)
    k = np.arange(mid)
    table[(mid - k) % mid, k] = 1.0
    return table


def parts(x):
    high = x.astype(jnp.bfloat16)
    low = (x - high.astype(jnp.float32)).astype(jnp.bfloat16)
    return high, low


def dot(a, b):
    return jnp.dot(a, b, preferred_element_type=jnp.float32)


def prepare_kernel(s_hbm, w_hbm, row_hbm, col_hbm, coef_ref, rt_ref, ct_ref, s_ref, w_ref, row_ref, col_ref, sems):
    half, side = w_ref.shape
    here = lax.axis_index("tile")
    swap = lax.axis_index("groups") % 2
    mine = pl.ds(pl.multiple_of(here * half, half), half)
    other = pl.ds(pl.multiple_of((1 - here) * half, half), half)
    moves = (
        (s_hbm, s_ref),
        (w_hbm.at[mine], w_ref),
        (row_hbm.at[mine], row_ref.at[pl.ds(0, half)]),
        (row_hbm.at[other], row_ref.at[pl.ds(half, half)]),
        (col_hbm, col_ref),
    )
    copies = [pltpu.make_async_copy(source, target, sems.at[n]) for n, (source, target) in enumerate(moves)]
    for copy in copies:
        copy.start()
    for copy in copies:
        copy.wait()
    w = w_ref[...]
    u, v = s_ref[swap] * w, s_ref[1 - swap] * w
    turn = (1 - 2 * swap).astype(jnp.float32)
    coef_ref[0], coef_ref[1], coef_ref[2], coef_ref[3] = u, v, u * turn, v * turn
    ct_ref[0], ct_ref[1] = parts(col_ref[...])
    odd = lax.broadcasted_iota(jnp.int32, (side, side), 0) % 2
    rt_ref[0], rt_ref[1] = parts(row_ref[...] * (1 - 2 * odd * here).astype(jnp.float32))


def correlate(a, b, coef_ref, col_ref, rt_ref, keep_ref, send_ref, n):
    half, side = a.shape
    mid = side // 2
    squares = jnp.sum((a * a + b * b).reshape(half // 8, 8, side), axis=0)
    power = jnp.broadcast_to(jnp.sum(squares), (keep_ref.shape[1] - half, side))
    z = jnp.concatenate([coef_ref[0] * a + coef_ref[1] * b, coef_ref[3] * a - coef_ref[2] * b], 0)
    zh, zl = parts(z)
    ch, cl = col_ref[0], col_ref[1]
    m = dot(zh, ch) + (dot(zl, ch) + dot(zh, cl))
    mcr, mci = m[:half, :mid], m[half:, :mid]
    msr, msi = m[:half, mid:], m[half:, mid:]
    first = lax.broadcasted_iota(jnp.int32, (half, mid), 1) == 0
    real = jnp.concatenate([mcr - jnp.where(first, 0.0, msi), jnp.where(first, msr, mcr + msi)], 1)
    imag = jnp.concatenate([mci + jnp.where(first, 0.0, msr), jnp.where(first, msi, mci - msr)], 1)
    ah, al = parts(jnp.concatenate([real, imag], 0))
    rh, rl = rt_ref[0], rt_ref[1]
    p = dot(rh, ah) + (dot(rh, al) + dot(rl, ah))
    keep_ref[n, :half] = p[:half]
    keep_ref[n, half:] = power
    send_ref[n, :half] = p[half:]
    send_ref[n, half:] = power


def maps_kernel(wholes, places, coef_ref, rt_ref, col_ref, *refs):
    inputs, (keep_ref, send_ref) = refs[:-2], refs[-2:]
    whole_refs, part_refs = inputs[:wholes], inputs[wholes:]
    swap = lax.axis_index("groups") % 2
    for n, ref in enumerate(whole_refs):
        correlate(ref[swap], ref[1 - swap], coef_ref, col_ref, rt_ref, keep_ref, send_ref, n)
    half = coef_ref.shape[1]
    first_core = lax.axis_index("tile") == 0

    def read(even, odd, row):
        here = part_refs[even][row:row + half]
        return here if even == odd else jnp.where(first_core, here, part_refs[odd][row:row + half])

    for n, (a, b) in enumerate(places):
        correlate(read(*a), read(*b), coef_ref, col_ref, rt_ref, keep_ref, send_ref, wholes + n)


def stats_kernel(calls, entries, *refs):
    keeps, recvs = refs[:calls], refs[calls:2 * calls]
    fold_ref, peak_ref, mean_ref, square_ref, flip_ref = refs[2 * calls:]
    half, side = peak_ref.shape[1:]
    mid = side // 2
    pairs = [(keep, recv, n) for keep, recv in zip(keeps, recvs) for n in range(keep.shape[0])]
    count = len(pairs)
    for block in range(half // 8):
        rows = pl.ds(block * 8, 8)
        best = total = squares = None
        for keep, recv, n in pairs:
            power = (keep[n, half:half + 8] + recv[n, half:half + 8]) * (1.0 / entries)
            scale = lax.rsqrt(power + 1e-6) * (1.0 / side)
            c = (keep[n, rows] + recv[n, rows]) * scale
            if best is None:
                best, total, squares = c, c, c * c
            else:
                best, total, squares = jnp.maximum(best, c), total + c, squares + c * c
        total = total * (1.0 / count)
        squares = squares * (1.0 / count)
        for n, (ref, value) in enumerate(((peak_ref, best), (mean_ref, total), (square_ref, squares))):
            ref[0, rows, :mid] = value[:, :mid]
            flip_ref[pl.ds(n * half + block * 8, 8)] = value[:, mid:]
    right = jnp.dot(flip_ref[...], fold_ref[...], precision=lax.Precision.HIGHEST, preferred_element_type=jnp.float32)
    for n, ref in enumerate((peak_ref, mean_ref, square_ref)):
        ref[0, :, mid:] = right[n * half:(n + 1) * half]


def flipped(x, axis, bits):
    return lax.ppermute(x, axis, [(i, i ^ bits) for i in range(lax.axis_size(axis))])


def crossed(x, even, odd):
    groups, orients, cores = (lax.axis_size(axis) for axis in ("groups", "orient", "tile"))
    pairs = []
    for g in range(groups):
        for o in range(orients):
            for c in range(cores):
                group_bits, orient_bits = odd if c else even
                pairs.append(((g * orients + o) * cores + c, ((g ^ group_bits) * orients + (o ^ orient_bits)) * cores + c))
    return lax.ppermute(x, ("groups", "orient", "tile"), pairs)


def shards(spectra, templates, weights):
    half, side = spectra.shape[2:]
    orients = lax.axis_size("orient")
    vmem = pl.BlockSpec(memory_space=pltpu.VMEM)
    hbm = pl.BlockSpec(memory_space=pltpu.HBM)
    params = pltpu.CompilerParams(vmem_limit_bytes=24 << 20)
    shape = lambda *dims, dtype=jnp.float32: jax.ShapeDtypeStruct(dims, dtype)
    scratch = lambda *dims: pltpu.VMEM(dims, jnp.float32)
    template = templates[0]

    coef, table, columns = pl.pallas_call(
        prepare_kernel,
        in_specs=[hbm] * 4,
        out_specs=[vmem] * 3,
        out_shape=[shape(4, half, side)] + [shape(2, side, side, dtype=jnp.bfloat16)] * 2,
        scratch_shapes=[
            scratch(2, half, side), scratch(half, side), scratch(side, side), scratch(side, side), pltpu.SemaphoreType.DMA((5,)),
        ],
        compiler_params=params,
        name="prepare",
    )(spectra[0], weights, jnp.asarray(row_table(side, half)), jnp.asarray(column_table(side)))

    def maps(wholes, arrays=(), places=(), extra=8):
        return pl.pallas_call(
            functools.partial(maps_kernel, len(wholes), places),
            in_specs=[vmem] * (3 + len(wholes) + len(arrays)),
            out_specs=[vmem] * 2,
            out_shape=[shape(len(wholes) + len(places), half + extra, side)] * 2,
            compiler_params=params,
            name="maps",
        )(coef, table, columns, *wholes, *arrays)

    if lax.axis_size("groups") == 2 and orients == 8:
        core = lax.axis_index("tile")
        part = lax.dynamic_index_in_dim(template, lax.axis_index("groups"), 0, keepdims=False)
        near1, near2 = (flipped(part, "orient", 2 * k) for k in (1, 2))
        beside = flipped(lax.optimization_barrier((template, part))[0], "orient", 1)
        near1, near2, beside = lax.optimization_barrier((near1, near2, beside))
        near = jnp.concatenate([near1, near2], 0)
        far = flipped(near2, "orient", 2)
        near_b = crossed(near, (0, 1), (1, 0))
        near_a = crossed(near, (1, 0), (0, 1))
        far, near_a, near_b, coef = lax.optimization_barrier((far, near_a, near_b, coef))
        rows = lambda x, n: lax.dynamic_slice_in_dim(x, n * half, half)
        corner = crossed(near_a[half:], (0, 3), (1, 2))
        last_b = crossed(jnp.concatenate([far, rows(near_a, 1 - core)], 0), (0, 1), (1, 0))
        last_a = crossed(jnp.concatenate([far, rows(near_b, core)], 0), (1, 0), (0, 1))
        early = maps(
            [template, beside],
            [near, near_a, near_b],
            (
                ((0, 0, 0), (1, 2, 0)),
                ((0, 0, half), (1, 2, half)),
            ),
            16,
        )
        last_a, last_b, corner, early = lax.optimization_barrier((last_a, last_b, corner, early))
        late = maps(
            [],
            [near_a, near_b, last_a, last_b, far, corner],
            (
                ((1, 0, 0), (2, 3, half)),
                ((1, 0, half), (3, 2, half)),
                ((4, 4, 0), (2, 3, 0)),
                ((3, 2, 0), (5, 5, 0)),
            ),
        )
        calls = [early, late]
    else:
        rest = [template] + [flipped(template, "orient", k) for k in range(1, orients)]
        calls = [maps(rest[i:i + 4]) for i in range(0, len(rest), 4)]
    keeps = [keep for keep, _ in calls]
    recvs = [flipped(send, "tile", 1) for _, send in calls]
    return tuple(pl.pallas_call(
        functools.partial(stats_kernel, len(keeps), 2 * side * side),
        in_specs=[vmem] * (2 * len(keeps) + 1),
        out_specs=[vmem] * 3,
        out_shape=[shape(1, half, side)] * 3,
        scratch_shapes=[scratch(3 * half, side // 2)],
        compiler_params=params,
        name="statistics",
    )(*keeps, *recvs, jnp.asarray(unfold_table(side // 2))))


def solution(mesh):
    in_specs = (
        P(("groups", "orient"), None, "tile", None),
        P("orient", None, "tile", None),
        P("groups", None),
    )
    out_specs = (P(("groups", "orient"), "tile", None),) * 3
    return jax.shard_map(shards, mesh=mesh, in_specs=in_specs, out_specs=out_specs, check_vma=False)
```

```python
import functools
import math

import jax
import jax.numpy as jnp
import numpy as np
from jax import lax
from jax.experimental import pallas as pl
from jax.experimental.pallas import tpu as pltpu
from jax.sharding import PartitionSpec as P


def column_table(side):
    mid = side // 2
    k = np.arange(side)[:, None]
    x = np.arange(mid)[None, :]
    angle = 2.0 * math.pi * (k * x % side) / side
    right = np.sin(angle)
    right[:, 0] = np.cos(math.pi * k[:, 0])
    return np.concatenate([np.cos(angle), right], 1).astype(np.float32)


def row_table(side, half):
    y = np.arange(side)[:, None]
    k = np.arange(half)[None, :]
    angle = 2.0 * math.pi * (k * y % side) / side
    return np.concatenate([np.cos(angle), -np.sin(angle)], 1).astype(np.float32)


def unfold_table(mid):
    table = np.zeros((mid, mid), np.float32)
    k = np.arange(mid)
    table[(mid - k) % mid, k] = 1.0
    return table


def parts(x):
    high = x.astype(jnp.bfloat16)
    low = (x - high.astype(jnp.float32)).astype(jnp.bfloat16)
    return high, low


def dot(a, b):
    return jnp.dot(a, b, preferred_element_type=jnp.float32)


def prepare_kernel(s_hbm, w_hbm, table_hbm, coef_ref, rt_ref, ct_ref, s_ref, w_ref, row_ref, col_ref, sems):
    half, side = w_ref.shape
    here = lax.axis_index("tile")
    swap = lax.axis_index("groups") % 2
    mine = pl.ds(pl.multiple_of(here * half, half), half)
    other = pl.ds(pl.multiple_of((1 - here) * half, half), half)
    moves = (
        (s_hbm, s_ref),
        (w_hbm.at[mine], w_ref),
        (table_hbm.at[0, mine], row_ref.at[pl.ds(0, half)]),
        (table_hbm.at[0, other], row_ref.at[pl.ds(half, half)]),
        (table_hbm.at[1], col_ref),
    )
    copies = [pltpu.make_async_copy(source, target, sems.at[n]) for n, (source, target) in enumerate(moves)]
    for copy in copies:
        copy.start()
    for copy in copies:
        copy.wait()
    w = w_ref[...]
    u, v = s_ref[swap] * w, s_ref[1 - swap] * w
    turn = (1 - 2 * swap).astype(jnp.float32)
    coef_ref[0], coef_ref[1], coef_ref[2], coef_ref[3] = u, v, u * turn, v * turn
    ct_ref[0], ct_ref[1] = parts(col_ref[...])
    odd = lax.broadcasted_iota(jnp.int32, (side, side), 0) % 2
    rt_ref[0], rt_ref[1] = parts(row_ref[...] * (1 - 2 * odd * here).astype(jnp.float32))


def correlate(a, b, coef_ref, col_ref, rt_ref, keep_ref, send_ref, n):
    half, side = a.shape
    mid = side // 2
    squares = jnp.sum((a * a + b * b).reshape(half // 8, 8, side), axis=0)
    power = jnp.broadcast_to(jnp.sum(squares), (keep_ref.shape[1] - half, side))
    z = jnp.concatenate([coef_ref[0] * a + coef_ref[1] * b, coef_ref[3] * a - coef_ref[2] * b], 0)
    zh, zl = parts(z)
    ch, cl = col_ref[0], col_ref[1]
    m = dot(zh, ch) + (dot(zl, ch) + dot(zh, cl))
    mcr, mci = m[:half, :mid], m[half:, :mid]
    msr, msi = m[:half, mid:], m[half:, mid:]
    first = lax.broadcasted_iota(jnp.int32, (half, mid), 1) == 0
    real = jnp.concatenate([mcr - jnp.where(first, 0.0, msi), jnp.where(first, msr, mcr + msi)], 1)
    imag = jnp.concatenate([mci + jnp.where(first, 0.0, msr), jnp.where(first, msi, mci - msr)], 1)
    ah, al = parts(jnp.concatenate([real, imag], 0))
    rh, rl = rt_ref[0], rt_ref[1]
    p = dot(rh, ah) + (dot(rh, al) + dot(rl, ah))
    keep_ref[n, :half] = p[:half]
    keep_ref[n, half:] = power
    send_ref[n, :half] = p[half:]
    send_ref[n, half:] = power


def maps_kernel(wholes, places, coef_ref, rt_ref, col_ref, *refs):
    inputs, (keep_ref, send_ref) = refs[:-2], refs[-2:]
    whole_refs, part_refs = inputs[:wholes], inputs[wholes:]
    swap = lax.axis_index("groups") % 2
    for n, ref in enumerate(whole_refs):
        correlate(ref[swap], ref[1 - swap], coef_ref, col_ref, rt_ref, keep_ref, send_ref, n)
    half = coef_ref.shape[1]
    for n, pair in enumerate(places):
        a, b = (part_refs[array][row:row + half] for array, row in pair)
        correlate(a, b, coef_ref, col_ref, rt_ref, keep_ref, send_ref, wholes + n)


def stats_kernel(calls, entries, *refs):
    keeps, recvs = refs[:calls], refs[calls:2 * calls]
    fold_ref, peak_ref, mean_ref, square_ref, flip_ref = refs[2 * calls:]
    half, side = peak_ref.shape[1:]
    mid = side // 2
    pairs = [(keep, recv, n) for keep, recv in zip(keeps, recvs) for n in range(keep.shape[0])]
    count = len(pairs)
    for block in range(half // 8):
        rows = pl.ds(block * 8, 8)
        best = total = squares = None
        for keep, recv, n in pairs:
            power = (keep[n, half:half + 8] + recv[n, half:half + 8]) * (1.0 / entries)
            scale = lax.rsqrt(power + 1e-6) * (1.0 / side)
            c = (keep[n, rows] + recv[n, rows]) * scale
            if best is None:
                best, total, squares = c, c, c * c
            else:
                best, total, squares = jnp.maximum(best, c), total + c, squares + c * c
        total = total * (1.0 / count)
        squares = squares * (1.0 / count)
        for n, (ref, value) in enumerate(((peak_ref, best), (mean_ref, total), (square_ref, squares))):
            ref[0, rows, :mid] = value[:, :mid]
            flip_ref[pl.ds(n * half + block * 8, 8)] = value[:, mid:]
    right = jnp.dot(flip_ref[...], fold_ref[...], precision=lax.Precision.HIGHEST, preferred_element_type=jnp.float32)
    for n, ref in enumerate((peak_ref, mean_ref, square_ref)):
        ref[0, :, mid:] = right[n * half:(n + 1) * half]


def flipped(x, axis, bits):
    return lax.ppermute(x, axis, [(i, i ^ bits) for i in range(lax.axis_size(axis))])


def shards(spectra, templates, weights):
    half, side = spectra.shape[2:]
    orients = lax.axis_size("orient")
    vmem = pl.BlockSpec(memory_space=pltpu.VMEM)
    hbm = pl.BlockSpec(memory_space=pltpu.HBM)
    params = pltpu.CompilerParams(vmem_limit_bytes=24 << 20)
    shape = lambda *dims, dtype=jnp.float32: jax.ShapeDtypeStruct(dims, dtype)
    scratch = lambda *dims: pltpu.VMEM(dims, jnp.float32)
    template = templates[0]

    coef, table, columns = pl.pallas_call(
        prepare_kernel,
        in_specs=[hbm] * 3,
        out_specs=[vmem] * 3,
        out_shape=[shape(4, half, side)] + [shape(2, side, side, dtype=jnp.bfloat16)] * 2,
        scratch_shapes=[
            scratch(2, half, side), scratch(half, side), scratch(side, side), scratch(side, side), pltpu.SemaphoreType.DMA((5,)),
        ],
        compiler_params=params,
        name="prepare",
    )(spectra[0], weights, jnp.asarray(np.stack([row_table(side, half), column_table(side)])))

    def maps(wholes, arrays=(), places=(), extra=8):
        return pl.pallas_call(
            functools.partial(maps_kernel, len(wholes), places),
            in_specs=[vmem] * (3 + len(wholes) + len(arrays)),
            out_specs=[vmem] * 2,
            out_shape=[shape(len(wholes) + len(places), half + extra, side)] * 2,
            compiler_params=params,
            name="maps",
        )(coef, table, columns, *wholes, *arrays)

    if lax.axis_size("groups") == 2 and orients == 8:
        plane = lax.axis_index("groups")
        pick = lambda whole, n: lax.dynamic_index_in_dim(whole, n, 0, keepdims=False)
        part = pick(template, plane)
        near1, near2 = (flipped(part, "orient", 2 * k) for k in (1, 2))
        beside = flipped(lax.optimization_barrier((template, part))[0], "orient", 1)
        near1, near2, beside = lax.optimization_barrier((near1, near2, beside))
        near = jnp.concatenate([near1, near2], 0)
        far = flipped(jnp.concatenate([near2, pick(beside, 1 - plane)], 0), "orient", 2)
        near_x = flipped(near, "groups", 1)
        near_y = flipped(near, "orient", 1)
        far, near_x, near_y, coef = lax.optimization_barrier((far, near_x, near_y, coef))
        last_x = flipped(jnp.concatenate([far[:half], near_y[half:]], 0), "groups", 1)
        corner = flipped(near_x[half:], "orient", 3)
        last_y = flipped(far[:half], "orient", 1)
        early = maps([template, beside], [near, near_x], (((0, 0), (1, 0)), ((0, half), (1, half))), 16)
        last_x, last_y, corner, early = lax.optimization_barrier((last_x, last_y, corner, early))
        late = maps(
            [],
            [near_y, last_x, last_y, far, corner],
            (
                ((0, 0), (3, half)),
                ((0, half), (1, half)),
                ((3, 0), (1, 0)),
                ((2, 0), (4, 0)),
            ),
        )
        calls = [early, late]
    else:
        rest = [template] + [flipped(template, "orient", k) for k in range(1, orients)]
        calls = [maps(rest[i:i + 4]) for i in range(0, len(rest), 4)]
    keeps = [keep for keep, _ in calls]
    recvs = [flipped(send, "tile", 1) for _, send in calls]
    return tuple(pl.pallas_call(
        functools.partial(stats_kernel, len(keeps), 2 * side * side),
        in_specs=[vmem] * (2 * len(keeps) + 1),
        out_specs=[vmem] * 3,
        out_shape=[shape(1, half, side)] * 3,
        scratch_shapes=[scratch(3 * half, side // 2)],
        compiler_params=params,
        name="statistics",
    )(*keeps, *recvs, jnp.asarray(unfold_table(side // 2))))


def solution(mesh):
    in_specs = (
        P(("groups", "orient"), None, "tile", None),
        P("orient", None, "tile", None),
        P("groups", None),
    )
    out_specs = (P(("groups", "orient"), "tile", None),) * 3
    return jax.shard_map(shards, mesh=mesh, in_specs=in_specs, out_specs=out_specs, check_vma=False)
```

```python
import functools
import math

import jax
import jax.numpy as jnp
import numpy as np
from jax import lax
from jax.experimental import pallas as pl
from jax.experimental.pallas import tpu as pltpu
from jax.sharding import PartitionSpec as P


def column_table(side):
    mid = side // 2
    k = np.arange(side)[:, None]
    x = np.arange(mid)[None, :]
    angle = 2.0 * math.pi * (k * x % side) / side
    right = np.sin(angle)
    right[:, 0] = np.cos(math.pi * k[:, 0])
    return np.concatenate([np.cos(angle), right], 1).astype(np.float32)


def row_table(side, half):
    y = np.arange(side)[:, None]
    k = np.arange(half)[None, :]
    angle = 2.0 * math.pi * (k * y % side) / side
    return np.concatenate([np.cos(angle), -np.sin(angle)], 1).astype(np.float32)


def unfold_table(mid):
    table = np.zeros((mid, mid), np.float32)
    k = np.arange(mid)
    table[(mid - k) % mid, k] = 1.0
    return table


def parts(x):
    high = x.astype(jnp.bfloat16)
    low = (x - high.astype(jnp.float32)).astype(jnp.bfloat16)
    return high, low


def dot(a, b):
    return jnp.dot(a, b, preferred_element_type=jnp.float32)


def prepare_kernel(s_hbm, w_hbm, table_hbm, coef_ref, rt_ref, ct_ref, s_ref, w_ref, row_ref, col_ref, sems):
    half, side = w_ref.shape
    here = lax.axis_index("tile")
    swap = lax.axis_index("groups") % 2
    mine = pl.ds(pl.multiple_of(here * half, half), half)
    other = pl.ds(pl.multiple_of((1 - here) * half, half), half)
    moves = (
        (s_hbm, s_ref),
        (w_hbm.at[mine], w_ref),
        (table_hbm.at[0, mine], row_ref.at[pl.ds(0, half)]),
        (table_hbm.at[0, other], row_ref.at[pl.ds(half, half)]),
        (table_hbm.at[1], col_ref),
    )
    copies = [pltpu.make_async_copy(source, target, sems.at[n]) for n, (source, target) in enumerate(moves)]
    for copy in copies:
        copy.start()
    for copy in copies:
        copy.wait()
    w = w_ref[...]
    u, v = s_ref[swap] * w, s_ref[1 - swap] * w
    turn = (1 - 2 * swap).astype(jnp.float32)
    coef_ref[0], coef_ref[1], coef_ref[2], coef_ref[3] = u, v, u * turn, v * turn
    ct_ref[0], ct_ref[1] = parts(col_ref[...])
    odd = lax.broadcasted_iota(jnp.int32, (side, side), 0) % 2
    rt_ref[0], rt_ref[1] = parts(row_ref[...] * (1 - 2 * odd * here).astype(jnp.float32))


def correlate(a, b, coef_ref, col_ref, rt_ref, keep_ref, send_ref, n):
    half, side = a.shape
    mid = side // 2
    squares = jnp.sum((a * a + b * b).reshape(half // 8, 8, side), axis=0)
    power = jnp.broadcast_to(jnp.sum(squares), (keep_ref.shape[1] - half, side))
    z = jnp.concatenate([coef_ref[0] * a + coef_ref[1] * b, coef_ref[3] * a - coef_ref[2] * b], 0)
    zh, zl = parts(z)
    ch, cl = col_ref[0], col_ref[1]
    m = dot(zh, ch) + (dot(zl, ch) + dot(zh, cl))
    mcr, mci = m[:half, :mid], m[half:, :mid]
    msr, msi = m[:half, mid:], m[half:, mid:]
    first = lax.broadcasted_iota(jnp.int32, (half, mid), 1) == 0
    real = jnp.concatenate([mcr - jnp.where(first, 0.0, msi), jnp.where(first, msr, mcr + msi)], 1)
    imag = jnp.concatenate([mci + jnp.where(first, 0.0, msr), jnp.where(first, msi, mci - msr)], 1)
    ah, al = parts(jnp.concatenate([real, imag], 0))
    rh, rl = rt_ref[0], rt_ref[1]
    p = dot(rh, ah) + (dot(rh, al) + dot(rl, ah))
    keep_ref[n, :half] = p[:half]
    keep_ref[n, half:] = power
    send_ref[n, :half] = p[half:]
    send_ref[n, half:] = power


def maps_kernel(wholes, places, coef_ref, rt_ref, col_ref, *refs):
    inputs, (keep_ref, send_ref) = refs[:-2], refs[-2:]
    whole_refs, part_refs = inputs[:wholes], inputs[wholes:]
    swap = lax.axis_index("groups") % 2
    for n, ref in enumerate(whole_refs):
        correlate(ref[swap], ref[1 - swap], coef_ref, col_ref, rt_ref, keep_ref, send_ref, n)
    for n, pair in enumerate(places):
        a, b = (jnp.concatenate([part_refs[array][start:stop] for array, start, stop in pieces], 0) for pieces in pair)
        correlate(a, b, coef_ref, col_ref, rt_ref, keep_ref, send_ref, wholes + n)


def stats_kernel(calls, entries, *refs):
    keeps, recvs = refs[:calls], refs[calls:2 * calls]
    fold_ref, peak_ref, mean_ref, square_ref, flip_ref = refs[2 * calls:]
    half, side = peak_ref.shape[1:]
    mid = side // 2
    pairs = [(keep, recv, n) for keep, recv in zip(keeps, recvs) for n in range(keep.shape[0])]
    count = len(pairs)
    for block in range(half // 8):
        rows = pl.ds(block * 8, 8)
        best = total = squares = None
        for keep, recv, n in pairs:
            power = (keep[n, half:half + 8] + recv[n, half:half + 8]) * (1.0 / entries)
            scale = lax.rsqrt(power + 1e-6) * (1.0 / side)
            c = (keep[n, rows] + recv[n, rows]) * scale
            if best is None:
                best, total, squares = c, c, c * c
            else:
                best, total, squares = jnp.maximum(best, c), total + c, squares + c * c
        total = total * (1.0 / count)
        squares = squares * (1.0 / count)
        for n, (ref, value) in enumerate(((peak_ref, best), (mean_ref, total), (square_ref, squares))):
            ref[0, rows, :mid] = value[:, :mid]
            flip_ref[pl.ds(n * half + block * 8, 8)] = value[:, mid:]
    right = jnp.dot(flip_ref[...], fold_ref[...], precision=lax.Precision.HIGHEST, preferred_element_type=jnp.float32)
    for n, ref in enumerate((peak_ref, mean_ref, square_ref)):
        ref[0, :, mid:] = right[n * half:(n + 1) * half]


def flipped(x, axis, bits):
    return lax.ppermute(x, axis, [(i, i ^ bits) for i in range(lax.axis_size(axis))])


def shards(spectra, templates, weights):
    half, side = spectra.shape[2:]
    orients = lax.axis_size("orient")
    vmem = pl.BlockSpec(memory_space=pltpu.VMEM)
    hbm = pl.BlockSpec(memory_space=pltpu.HBM)
    params = pltpu.CompilerParams(vmem_limit_bytes=24 << 20)
    shape = lambda *dims, dtype=jnp.float32: jax.ShapeDtypeStruct(dims, dtype)
    scratch = lambda *dims: pltpu.VMEM(dims, jnp.float32)
    template = templates[0]

    coef, table, columns = pl.pallas_call(
        prepare_kernel,
        in_specs=[hbm] * 3,
        out_specs=[vmem] * 3,
        out_shape=[shape(4, half, side)] + [shape(2, side, side, dtype=jnp.bfloat16)] * 2,
        scratch_shapes=[
            scratch(2, half, side), scratch(half, side), scratch(side, side), scratch(side, side), pltpu.SemaphoreType.DMA((5,)),
        ],
        compiler_params=params,
        name="prepare",
    )(spectra[0], weights, jnp.asarray(np.stack([row_table(side, half), column_table(side)])))

    def maps(wholes, arrays=(), places=(), extra=8):
        return pl.pallas_call(
            functools.partial(maps_kernel, len(wholes), places),
            in_specs=[vmem] * (3 + len(wholes) + len(arrays)),
            out_specs=[vmem] * 2,
            out_shape=[shape(len(wholes) + len(places), half + extra, side)] * 2,
            compiler_params=params,
            name="maps",
        )(coef, table, columns, *wholes, *arrays)

    if lax.axis_size("groups") == 2 and orients == 8:
        plane = lax.axis_index("groups")
        most = half - 8
        part, rest = (lax.dynamic_index_in_dim(template, n, 0, keepdims=False) for n in (plane, 1 - plane))
        near1, near2 = (flipped(part, "orient", 2 * k) for k in (1, 2))
        beside = flipped(rest[:most], "orient", 1)
        beside, near1, near2 = lax.optimization_barrier((beside, near1, near2))
        near = jnp.concatenate([near1, near2], 0)
        near_y = flipped(jnp.concatenate([near1, near2, part, rest[most:]], 0), "orient", 1)
        near_x = flipped(near, "groups", 1)
        far = flipped(jnp.concatenate([near2, beside], 0), "orient", 2)
        far, near_x, near_y, coef = lax.optimization_barrier((far, near_x, near_y, coef))
        last_x = flipped(jnp.concatenate([far[:half], near_y[half:side - 8], near_y[most:half]], 0), "groups", 1)
        last_y = flipped(jnp.concatenate([far[:half], near_x[side - 8:]], 0), "orient", 1)
        corner = flipped(near_x[half:], "orient", 3)
        block = lambda array, start=0, rows=half: ((array, start, start + rows),)
        early = maps(
            [],
            [part, rest, near_y, beside, near, near_x],
            (
                (block(0), block(1)),
                (block(2, side), block(3, 0, most) + block(2, side + half, 8)),
                (block(4), block(5)),
                (block(4, half), block(5, half)),
            ),
            16,
        )
        last_x, last_y, corner, early = lax.optimization_barrier((last_x, last_y, corner, early))
        late = maps(
            [],
            [near_y, last_x, last_y, far, corner],
            (
                (block(0), block(3, half, most) + block(1, side - 8, 8)),
                (block(0, half), block(1, half, most) + block(2, half, 8)),
                (block(3), block(1)),
                (block(2), block(4)),
            ),
        )
        calls = [early, late]
    else:
        rest = [template] + [flipped(template, "orient", k) for k in range(1, orients)]
        calls = [maps(rest[i:i + 4]) for i in range(0, len(rest), 4)]
    keeps = [keep for keep, _ in calls]
    recvs = [flipped(send, "tile", 1) for _, send in calls]
    return tuple(pl.pallas_call(
        functools.partial(stats_kernel, len(keeps), 2 * side * side),
        in_specs=[vmem] * (2 * len(keeps) + 1),
        out_specs=[vmem] * 3,
        out_shape=[shape(1, half, side)] * 3,
        scratch_shapes=[scratch(3 * half, side // 2)],
        compiler_params=params,
        name="statistics",
    )(*keeps, *recvs, jnp.asarray(unfold_table(side // 2))))


def solution(mesh):
    in_specs = (
        P(("groups", "orient"), None, "tile", None),
        P("orient", None, "tile", None),
        P("groups", None),
    )
    out_specs = (P(("groups", "orient"), "tile", None),) * 3
    return jax.shard_map(shards, mesh=mesh, in_specs=in_specs, out_specs=out_specs, check_vma=False)
```

```python
import functools
import math

import jax
import jax.numpy as jnp
import numpy as np
from jax import lax
from jax.experimental import pallas as pl
from jax.experimental.pallas import tpu as pltpu
from jax.sharding import PartitionSpec as P


def column_table(side):
    mid = side // 2
    k = np.arange(side)[:, None]
    x = np.arange(mid)[None, :]
    angle = 2.0 * math.pi * (k * x % side) / side
    right = np.sin(angle)
    right[:, 0] = np.cos(math.pi * k[:, 0])
    return np.concatenate([np.cos(angle), right], 1).astype(np.float32)


def row_table(side, half):
    y = np.arange(side)[:, None]
    k = np.arange(half)[None, :]
    angle = 2.0 * math.pi * (k * y % side) / side
    return np.concatenate([np.cos(angle), -np.sin(angle)], 1).astype(np.float32)


def unfold_table(mid):
    table = np.zeros((mid, mid), np.float32)
    k = np.arange(mid)
    table[(mid - k) % mid, k] = 1.0
    return table


def parts(x):
    high = x.astype(jnp.bfloat16)
    low = (x - high.astype(jnp.float32)).astype(jnp.bfloat16)
    return high, low


def dot(a, b):
    return jnp.dot(a, b, preferred_element_type=jnp.float32)


def prepare_kernel(s_hbm, w_hbm, table_hbm, coef_ref, rt_ref, ct_ref, s_ref, w_ref, row_ref, col_ref, sems):
    half, side = w_ref.shape
    here = lax.axis_index("tile")
    swap = lax.axis_index("groups") % 2
    mine = pl.ds(pl.multiple_of(here * half, half), half)
    other = pl.ds(pl.multiple_of((1 - here) * half, half), half)
    moves = (
        (s_hbm, s_ref),
        (w_hbm.at[mine], w_ref),
        (table_hbm.at[0, mine], row_ref.at[pl.ds(0, half)]),
        (table_hbm.at[0, other], row_ref.at[pl.ds(half, half)]),
        (table_hbm.at[1], col_ref),
    )
    copies = [pltpu.make_async_copy(source, target, sems.at[n]) for n, (source, target) in enumerate(moves)]
    for copy in copies:
        copy.start()
    for copy in copies:
        copy.wait()
    w = w_ref[...]
    u, v = s_ref[swap] * w, s_ref[1 - swap] * w
    turn = (1 - 2 * swap).astype(jnp.float32)
    coef_ref[0], coef_ref[1], coef_ref[2], coef_ref[3] = u, v, u * turn, v * turn
    ct_ref[0], ct_ref[1] = parts(col_ref[...])
    odd = lax.broadcasted_iota(jnp.int32, (side, side), 0) % 2
    rt_ref[0], rt_ref[1] = parts(row_ref[...] * (1 - 2 * odd * here).astype(jnp.float32))


def correlate(a, b, coef_ref, col_ref, rt_ref, keep_ref, send_ref, n):
    half, side = a.shape
    mid = side // 2
    squares = jnp.sum((a * a + b * b).reshape(half // 8, 8, side), axis=0)
    power = jnp.broadcast_to(jnp.sum(squares), (keep_ref.shape[1] - half, side))
    z = jnp.concatenate([coef_ref[0] * a + coef_ref[1] * b, coef_ref[3] * a - coef_ref[2] * b], 0)
    zh, zl = parts(z)
    ch, cl = col_ref[0], col_ref[1]
    m = dot(zh, ch) + (dot(zl, ch) + dot(zh, cl))
    mcr, mci = m[:half, :mid], m[half:, :mid]
    msr, msi = m[:half, mid:], m[half:, mid:]
    first = lax.broadcasted_iota(jnp.int32, (half, mid), 1) == 0
    real = jnp.concatenate([mcr - jnp.where(first, 0.0, msi), jnp.where(first, msr, mcr + msi)], 1)
    imag = jnp.concatenate([mci + jnp.where(first, 0.0, msr), jnp.where(first, msi, mci - msr)], 1)
    ah, al = parts(jnp.concatenate([real, imag], 0))
    rh, rl = rt_ref[0], rt_ref[1]
    p = dot(rh, ah) + (dot(rh, al) + dot(rl, ah))
    keep_ref[n, :half] = p[:half]
    keep_ref[n, half:] = power
    send_ref[n, :half] = p[half:]
    send_ref[n, half:] = power


def maps_kernel(wholes, places, coef_ref, rt_ref, col_ref, *refs):
    inputs, (keep_ref, send_ref) = refs[:-2], refs[-2:]
    whole_refs, part_refs = inputs[:wholes], inputs[wholes:]
    swap = lax.axis_index("groups") % 2
    for n, ref in enumerate(whole_refs):
        correlate(ref[swap], ref[1 - swap], coef_ref, col_ref, rt_ref, keep_ref, send_ref, n)
    for n, pair in enumerate(places):
        a, b = (jnp.concatenate([part_refs[array][start:stop] for array, start, stop in pieces], 0) for pieces in pair)
        correlate(a, b, coef_ref, col_ref, rt_ref, keep_ref, send_ref, wholes + n)


def stats_kernel(calls, entries, *refs):
    keeps, recvs = refs[:calls], refs[calls:2 * calls]
    fold_ref, peak_ref, mean_ref, square_ref, flip_ref = refs[2 * calls:]
    half, side = peak_ref.shape[1:]
    mid = side // 2
    pairs = [(keep, recv, n) for keep, recv in zip(keeps, recvs) for n in range(keep.shape[0])]
    count = len(pairs)
    for block in range(half // 8):
        rows = pl.ds(block * 8, 8)
        best = total = squares = None
        for keep, recv, n in pairs:
            power = (keep[n, half:half + 8] + recv[n, half:half + 8]) * (1.0 / entries)
            scale = lax.rsqrt(power + 1e-6) * (1.0 / side)
            c = (keep[n, rows] + recv[n, rows]) * scale
            if best is None:
                best, total, squares = c, c, c * c
            else:
                best, total, squares = jnp.maximum(best, c), total + c, squares + c * c
        total = total * (1.0 / count)
        squares = squares * (1.0 / count)
        for n, (ref, value) in enumerate(((peak_ref, best), (mean_ref, total), (square_ref, squares))):
            ref[0, rows, :mid] = value[:, :mid]
            flip_ref[pl.ds(n * half + block * 8, 8)] = value[:, mid:]
    right = jnp.dot(flip_ref[...], fold_ref[...], precision=lax.Precision.HIGHEST, preferred_element_type=jnp.float32)
    for n, ref in enumerate((peak_ref, mean_ref, square_ref)):
        ref[0, :, mid:] = right[n * half:(n + 1) * half]


def flipped(x, axis, bits):
    return lax.ppermute(x, axis, [(i, i ^ bits) for i in range(lax.axis_size(axis))])


def shards(spectra, templates, weights):
    half, side = spectra.shape[2:]
    orients = lax.axis_size("orient")
    vmem = pl.BlockSpec(memory_space=pltpu.VMEM)
    hbm = pl.BlockSpec(memory_space=pltpu.HBM)
    params = pltpu.CompilerParams(vmem_limit_bytes=24 << 20)
    shape = lambda *dims, dtype=jnp.float32: jax.ShapeDtypeStruct(dims, dtype)
    scratch = lambda *dims: pltpu.VMEM(dims, jnp.float32)
    template = templates[0]

    coef, table, columns = pl.pallas_call(
        prepare_kernel,
        in_specs=[hbm] * 3,
        out_specs=[vmem] * 3,
        out_shape=[shape(4, half, side)] + [shape(2, side, side, dtype=jnp.bfloat16)] * 2,
        scratch_shapes=[
            scratch(2, half, side), scratch(half, side), scratch(side, side), scratch(side, side), pltpu.SemaphoreType.DMA((5,)),
        ],
        compiler_params=params,
        name="prepare",
    )(spectra[0], weights, jnp.asarray(np.stack([row_table(side, half), column_table(side)])))

    def maps(wholes, arrays=(), places=(), extra=8):
        return pl.pallas_call(
            functools.partial(maps_kernel, len(wholes), places),
            in_specs=[vmem] * (3 + len(wholes) + len(arrays)),
            out_specs=[vmem] * 2,
            out_shape=[shape(len(wholes) + len(places), half + extra, side)] * 2,
            compiler_params=params,
            name="maps",
        )(coef, table, columns, *wholes, *arrays)

    if lax.axis_size("groups") == 2 and orients == 8:
        plane = lax.axis_index("groups")
        cut, most = half // 2, half - 8
        pick = lambda whole, n: lax.dynamic_index_in_dim(whole, n, 0, keepdims=False)
        part = pick(template, plane)
        near1, near2 = (flipped(part, "orient", 2 * k) for k in (1, 2))
        beside = flipped(lax.optimization_barrier((template, part))[0], "orient", 1)
        near1, near2, beside = lax.optimization_barrier((near1, near2, beside))
        near = jnp.concatenate([near1, near2], 0)
        far = flipped(jnp.concatenate([near2, pick(beside, 1 - plane)[:cut]], 0), "orient", 2)
        near_x = flipped(near, "groups", 1)
        near_y = flipped(near, "orient", 1)
        far, near_x, near_y, coef = lax.optimization_barrier((far, near_x, near_y, coef))
        last_x = flipped(jnp.concatenate([far[:half], near_y[half:side - 8], near_y[cut:half]], 0), "groups", 1)
        last_y = flipped(jnp.concatenate([far[:half], near_x[side - 8:]], 0), "orient", 1)
        corner = flipped(near_x[half:], "orient", 3)
        block = lambda array, start=0, rows=half: ((array, start, start + rows),)
        early = maps([template, beside], [near, near_x], ((block(0), block(1)), (block(0, half), block(1, half))), 16)
        last_x, last_y, corner, early = lax.optimization_barrier((last_x, last_y, corner, early))
        late = maps(
            [],
            [near_y, last_x, last_y, far, corner],
            (
                (block(0), block(3, half, cut) + block(1, side - 8, cut)),
                (block(0, half), block(1, half, most) + block(2, half, 8)),
                (block(3), block(1)),
                (block(2), block(4)),
            ),
        )
        calls = [early, late]
    else:
        rest = [template] + [flipped(template, "orient", k) for k in range(1, orients)]
        calls = [maps(rest[i:i + 4]) for i in range(0, len(rest), 4)]
    keeps = [keep for keep, _ in calls]
    recvs = [flipped(send, "tile", 1) for _, send in calls]
    return tuple(pl.pallas_call(
        functools.partial(stats_kernel, len(keeps), 2 * side * side),
        in_specs=[vmem] * (2 * len(keeps) + 1),
        out_specs=[vmem] * 3,
        out_shape=[shape(1, half, side)] * 3,
        scratch_shapes=[scratch(3 * half, side // 2)],
        compiler_params=params,
        name="statistics",
    )(*keeps, *recvs, jnp.asarray(unfold_table(side // 2))))


def solution(mesh):
    in_specs = (
        P(("groups", "orient"), None, "tile", None),
        P("orient", None, "tile", None),
        P("groups", None),
    )
    out_specs = (P(("groups", "orient"), "tile", None),) * 3
    return jax.shard_map(shards, mesh=mesh, in_specs=in_specs, out_specs=out_specs, check_vma=False)
```

```python
import functools
import math

import jax
import jax.numpy as jnp
import numpy as np
from jax import lax
from jax.experimental import pallas as pl
from jax.experimental.pallas import tpu as pltpu
from jax.sharding import PartitionSpec as P


def column_table(side):
    mid = side // 2
    k = np.arange(side)[:, None]
    x = np.arange(mid)[None, :]
    angle = 2.0 * math.pi * (k * x % side) / side
    right = np.sin(angle)
    right[:, 0] = np.cos(math.pi * k[:, 0])
    return np.concatenate([np.cos(angle), right], 1).astype(np.float32)


def row_table(side, half):
    y = np.arange(side)[:, None]
    k = np.arange(half)[None, :]
    angle = 2.0 * math.pi * (k * y % side) / side
    return np.concatenate([np.cos(angle), -np.sin(angle)], 1).astype(np.float32)


def unfold_table(mid):
    table = np.zeros((mid, mid), np.float32)
    k = np.arange(mid)
    table[(mid - k) % mid, k] = 1.0
    return table


def parts(x):
    high = x.astype(jnp.bfloat16)
    low = (x - high.astype(jnp.float32)).astype(jnp.bfloat16)
    return high, low


def dot(a, b):
    return jnp.dot(a, b, preferred_element_type=jnp.float32)


def prepare_kernel(s_hbm, w_hbm, table_hbm, coef_ref, rt_ref, ct_ref, s_ref, w_ref, row_ref, col_ref, sems):
    half, side = w_ref.shape
    here = lax.axis_index("tile")
    swap = lax.axis_index("groups") % 2
    mine = pl.ds(pl.multiple_of(here * half, half), half)
    other = pl.ds(pl.multiple_of((1 - here) * half, half), half)
    moves = (
        (s_hbm, s_ref),
        (w_hbm.at[mine], w_ref),
        (table_hbm.at[0, mine], row_ref.at[pl.ds(0, half)]),
        (table_hbm.at[0, other], row_ref.at[pl.ds(half, half)]),
        (table_hbm.at[1], col_ref),
    )
    copies = [pltpu.make_async_copy(source, target, sems.at[n]) for n, (source, target) in enumerate(moves)]
    for copy in copies:
        copy.start()
    for copy in copies:
        copy.wait()
    w = w_ref[...]
    u, v = s_ref[swap] * w, s_ref[1 - swap] * w
    turn = (1 - 2 * swap).astype(jnp.float32)
    coef_ref[0], coef_ref[1], coef_ref[2], coef_ref[3] = u, v, u * turn, v * turn
    ct_ref[0], ct_ref[1] = parts(col_ref[...])
    odd = lax.broadcasted_iota(jnp.int32, (side, side), 0) % 2
    rt_ref[0], rt_ref[1] = parts(row_ref[...] * (1 - 2 * odd * here).astype(jnp.float32))


def correlate(a, b, coef_ref, col_ref, rt_ref, keep_ref, send_ref, n):
    half, side = a.shape
    mid = side // 2
    squares = jnp.sum((a * a + b * b).reshape(half // 8, 8, side), axis=0)
    power = jnp.broadcast_to(jnp.sum(squares), (keep_ref.shape[1] - half, side))
    z = jnp.concatenate([coef_ref[0] * a + coef_ref[1] * b, coef_ref[3] * a - coef_ref[2] * b], 0)
    zh, zl = parts(z)
    ch, cl = col_ref[0], col_ref[1]
    m = dot(zh, ch) + (dot(zl, ch) + dot(zh, cl))
    mcr, mci = m[:half, :mid], m[half:, :mid]
    msr, msi = m[:half, mid:], m[half:, mid:]
    first = lax.broadcasted_iota(jnp.int32, (half, mid), 1) == 0
    real = jnp.concatenate([mcr - jnp.where(first, 0.0, msi), jnp.where(first, msr, mcr + msi)], 1)
    imag = jnp.concatenate([mci + jnp.where(first, 0.0, msr), jnp.where(first, msi, mci - msr)], 1)
    ah, al = parts(jnp.concatenate([real, imag], 0))
    rh, rl = rt_ref[0], rt_ref[1]
    p = dot(rh, ah) + (dot(rh, al) + dot(rl, ah))
    keep_ref[n, :half] = p[:half]
    keep_ref[n, half:] = power
    send_ref[n, :half] = p[half:]
    send_ref[n, half:] = power


def maps_kernel(wholes, places, coef_ref, rt_ref, col_ref, *refs):
    inputs, (keep_ref, send_ref) = refs[:-2], refs[-2:]
    whole_refs, part_refs = inputs[:wholes], inputs[wholes:]
    swap = lax.axis_index("groups") % 2
    for n, ref in enumerate(whole_refs):
        correlate(ref[swap], ref[1 - swap], coef_ref, col_ref, rt_ref, keep_ref, send_ref, n)
    for n, pair in enumerate(places):
        a, b = (jnp.concatenate([part_refs[array][start:stop] for array, start, stop in pieces], 0) for pieces in pair)
        correlate(a, b, coef_ref, col_ref, rt_ref, keep_ref, send_ref, wholes + n)


def stats_kernel(calls, entries, *refs):
    keeps, recvs = refs[:calls], refs[calls:2 * calls]
    fold_ref, peak_ref, mean_ref, square_ref, flip_ref = refs[2 * calls:]
    half, side = peak_ref.shape[1:]
    mid = side // 2
    pairs = [(keep, recv, n) for keep, recv in zip(keeps, recvs) for n in range(keep.shape[0])]
    count = len(pairs)
    for block in range(half // 8):
        rows = pl.ds(block * 8, 8)
        best = total = squares = None
        for keep, recv, n in pairs:
            power = (keep[n, half:half + 8] + recv[n, half:half + 8]) * (1.0 / entries)
            scale = lax.rsqrt(power + 1e-6) * (1.0 / side)
            c = (keep[n, rows] + recv[n, rows]) * scale
            if best is None:
                best, total, squares = c, c, c * c
            else:
                best, total, squares = jnp.maximum(best, c), total + c, squares + c * c
        total = total * (1.0 / count)
        squares = squares * (1.0 / count)
        for n, (ref, value) in enumerate(((peak_ref, best), (mean_ref, total), (square_ref, squares))):
            ref[0, rows, :mid] = value[:, :mid]
            flip_ref[pl.ds(n * half + block * 8, 8)] = value[:, mid:]
    right = jnp.dot(flip_ref[...], fold_ref[...], precision=lax.Precision.HIGHEST, preferred_element_type=jnp.float32)
    for n, ref in enumerate((peak_ref, mean_ref, square_ref)):
        ref[0, :, mid:] = right[n * half:(n + 1) * half]


def flipped(x, axis, bits):
    return lax.ppermute(x, axis, [(i, i ^ bits) for i in range(lax.axis_size(axis))])


def shards(spectra, templates, weights):
    half, side = spectra.shape[2:]
    orients = lax.axis_size("orient")
    vmem = pl.BlockSpec(memory_space=pltpu.VMEM)
    hbm = pl.BlockSpec(memory_space=pltpu.HBM)
    params = pltpu.CompilerParams(vmem_limit_bytes=24 << 20)
    shape = lambda *dims, dtype=jnp.float32: jax.ShapeDtypeStruct(dims, dtype)
    scratch = lambda *dims: pltpu.VMEM(dims, jnp.float32)
    template = templates[0]

    coef, table, columns = pl.pallas_call(
        prepare_kernel,
        in_specs=[hbm] * 3,
        out_specs=[vmem] * 3,
        out_shape=[shape(4, half, side)] + [shape(2, side, side, dtype=jnp.bfloat16)] * 2,
        scratch_shapes=[
            scratch(2, half, side), scratch(half, side), scratch(side, side), scratch(side, side), pltpu.SemaphoreType.DMA((5,)),
        ],
        compiler_params=params,
        name="prepare",
    )(spectra[0], weights, jnp.asarray(np.stack([row_table(side, half), column_table(side)])))

    def maps(wholes, arrays=(), places=(), extra=8):
        return pl.pallas_call(
            functools.partial(maps_kernel, len(wholes), places),
            in_specs=[vmem] * (3 + len(wholes) + len(arrays)),
            out_specs=[vmem] * 2,
            out_shape=[shape(len(wholes) + len(places), half + extra, side)] * 2,
            compiler_params=params,
            name="maps",
        )(coef, table, columns, *wholes, *arrays)

    if lax.axis_size("groups") == 2 and orients == 8:
        plane = lax.axis_index("groups")
        most = half - 8
        pick = lambda whole, n: lax.dynamic_index_in_dim(whole, n, 0, keepdims=False)
        part = pick(template, plane)
        near1, near2 = (flipped(part, "orient", 2 * k) for k in (1, 2))
        beside = flipped(lax.optimization_barrier((template, part))[0], "orient", 1)
        near1, near2, beside = lax.optimization_barrier((near1, near2, beside))
        near = jnp.concatenate([near1, near2], 0)
        far = flipped(jnp.concatenate([near2, pick(beside, 1 - plane)], 0), "orient", 2)
        near_x = flipped(near, "groups", 1)
        near_y = flipped(near, "orient", 1)
        far, near_x, near_y, coef = lax.optimization_barrier((far, near_x, near_y, coef))
        last_x = flipped(jnp.concatenate([far[:half], near_y[half:side - 8]], 0), "groups", 1)
        last_y = flipped(jnp.concatenate([far[:half], near_x[side - 8:]], 0), "orient", 1)
        corner = flipped(near_x[half:], "orient", 3)
        block = lambda array, start=0, rows=half: ((array, start, start + rows),)
        early = maps(
            [template, beside],
            [near, near_x, near_y, far],
            ((block(0), block(1)), (block(0, half), block(1, half)), (block(2), block(3, half))),
        )
        last_x, last_y, corner, early = lax.optimization_barrier((last_x, last_y, corner, early))
        late = maps(
            [],
            [near_y, last_x, last_y, far, corner],
            (
                (block(0, half), block(1, half, most) + block(2, half, 8)),
                (block(3), block(1)),
                (block(2), block(4)),
            ),
        )
        calls = [early, late]
    else:
        rest = [template] + [flipped(template, "orient", k) for k in range(1, orients)]
        calls = [maps(rest[i:i + 4]) for i in range(0, len(rest), 4)]
    keeps = [keep for keep, _ in calls]
    recvs = [flipped(send, "tile", 1) for _, send in calls]
    return tuple(pl.pallas_call(
        functools.partial(stats_kernel, len(keeps), 2 * side * side),
        in_specs=[vmem] * (2 * len(keeps) + 1),
        out_specs=[vmem] * 3,
        out_shape=[shape(1, half, side)] * 3,
        scratch_shapes=[scratch(3 * half, side // 2)],
        compiler_params=params,
        name="statistics",
    )(*keeps, *recvs, jnp.asarray(unfold_table(side // 2))))


def solution(mesh):
    in_specs = (
        P(("groups", "orient"), None, "tile", None),
        P("orient", None, "tile", None),
        P("groups", None),
    )
    out_specs = (P(("groups", "orient"), "tile", None),) * 3
    return jax.shard_map(shards, mesh=mesh, in_specs=in_specs, out_specs=out_specs, check_vma=False)
```

```python
import functools
import math

import jax
import jax.numpy as jnp
import numpy as np
from jax import lax
from jax.experimental import pallas as pl
from jax.experimental.pallas import tpu as pltpu
from jax.sharding import PartitionSpec as P


def column_table(side):
    mid = side // 2
    k = np.arange(side)[:, None]
    x = np.arange(mid)[None, :]
    angle = 2.0 * math.pi * (k * x % side) / side
    right = np.sin(angle)
    right[:, 0] = np.cos(math.pi * k[:, 0])
    return np.concatenate([np.cos(angle), right], 1).astype(np.float32)


def row_table(side, half):
    y = np.arange(side)[:, None]
    k = np.arange(half)[None, :]
    angle = 2.0 * math.pi * (k * y % side) / side
    return np.concatenate([np.cos(angle), -np.sin(angle)], 1).astype(np.float32)


def unfold_table(mid):
    table = np.zeros((mid, mid), np.float32)
    k = np.arange(mid)
    table[(mid - k) % mid, k] = 1.0
    return table


def parts(x):
    high = x.astype(jnp.bfloat16)
    low = (x - high.astype(jnp.float32)).astype(jnp.bfloat16)
    return high, low


def dot(a, b):
    return jnp.dot(a, b, preferred_element_type=jnp.float32)


def prepare_kernel(s_hbm, w_hbm, table_hbm, coef_ref, rt_ref, ct_ref, s_ref, w_ref, row_ref, col_ref, sems):
    half, side = w_ref.shape
    here = lax.axis_index("tile")
    swap = lax.axis_index("groups") % 2
    mine = pl.ds(pl.multiple_of(here * half, half), half)
    other = pl.ds(pl.multiple_of((1 - here) * half, half), half)
    moves = (
        (s_hbm, s_ref),
        (w_hbm.at[mine], w_ref),
        (table_hbm.at[0, mine], row_ref.at[pl.ds(0, half)]),
        (table_hbm.at[0, other], row_ref.at[pl.ds(half, half)]),
        (table_hbm.at[1], col_ref),
    )
    copies = [pltpu.make_async_copy(source, target, sems.at[n]) for n, (source, target) in enumerate(moves)]
    for copy in copies:
        copy.start()
    for copy in copies:
        copy.wait()
    w = w_ref[...]
    u, v = s_ref[swap] * w, s_ref[1 - swap] * w
    turn = (1 - 2 * swap).astype(jnp.float32)
    coef_ref[0], coef_ref[1], coef_ref[2], coef_ref[3] = u, v, u * turn, v * turn
    ct_ref[0], ct_ref[1] = parts(col_ref[...])
    odd = lax.broadcasted_iota(jnp.int32, (side, side), 0) % 2
    rt_ref[0], rt_ref[1] = parts(row_ref[...] * (1 - 2 * odd * here).astype(jnp.float32))


def correlate(a, b, coef_ref, col_ref, rt_ref, keep_ref, send_ref, n):
    half, side = a.shape
    mid = side // 2
    squares = jnp.sum((a * a + b * b).reshape(half // 8, 8, side), axis=0)
    power = jnp.broadcast_to(jnp.sum(squares), (keep_ref.shape[1] - half, side))
    z = jnp.concatenate([coef_ref[0] * a + coef_ref[1] * b, coef_ref[3] * a - coef_ref[2] * b], 0)
    zh, zl = parts(z)
    ch, cl = col_ref[0], col_ref[1]
    m = dot(zh, ch) + (dot(zl, ch) + dot(zh, cl))
    mcr, mci = m[:half, :mid], m[half:, :mid]
    msr, msi = m[:half, mid:], m[half:, mid:]
    first = lax.broadcasted_iota(jnp.int32, (half, mid), 1) == 0
    real = jnp.concatenate([mcr - jnp.where(first, 0.0, msi), jnp.where(first, msr, mcr + msi)], 1)
    imag = jnp.concatenate([mci + jnp.where(first, 0.0, msr), jnp.where(first, msi, mci - msr)], 1)
    ah, al = parts(jnp.concatenate([real, imag], 0))
    rh, rl = rt_ref[0], rt_ref[1]
    p = dot(rh, ah) + (dot(rh, al) + dot(rl, ah))
    keep_ref[n, :half] = p[:half]
    keep_ref[n, half:] = power
    send_ref[n, :half] = p[half:]
    send_ref[n, half:] = power


def maps_kernel(wholes, places, coef_ref, rt_ref, col_ref, *refs):
    inputs, (keep_ref, send_ref) = refs[:-2], refs[-2:]
    whole_refs, part_refs = inputs[:wholes], inputs[wholes:]
    swap = lax.axis_index("groups") % 2
    for n, ref in enumerate(whole_refs):
        correlate(ref[swap], ref[1 - swap], coef_ref, col_ref, rt_ref, keep_ref, send_ref, n)
    for n, pair in enumerate(places):
        a, b = (jnp.concatenate([part_refs[array][start:stop] for array, start, stop in pieces], 0) for pieces in pair)
        correlate(a, b, coef_ref, col_ref, rt_ref, keep_ref, send_ref, wholes + n)


def stats_kernel(calls, entries, *refs):
    keeps, recvs = refs[:calls], refs[calls:2 * calls]
    fold_ref, peak_ref, mean_ref, square_ref, flip_ref = refs[2 * calls:]
    half, side = peak_ref.shape[1:]
    mid = side // 2
    pairs = [(keep, recv, n) for keep, recv in zip(keeps, recvs) for n in range(keep.shape[0])]
    count = len(pairs)
    for block in range(half // 8):
        rows = pl.ds(block * 8, 8)
        best = total = squares = None
        for keep, recv, n in pairs:
            power = (keep[n, half:half + 8] + recv[n, half:half + 8]) * (1.0 / entries)
            scale = lax.rsqrt(power + 1e-6) * (1.0 / side)
            c = (keep[n, rows] + recv[n, rows]) * scale
            if best is None:
                best, total, squares = c, c, c * c
            else:
                best, total, squares = jnp.maximum(best, c), total + c, squares + c * c
        total = total * (1.0 / count)
        squares = squares * (1.0 / count)
        for n, (ref, value) in enumerate(((peak_ref, best), (mean_ref, total), (square_ref, squares))):
            ref[0, rows, :mid] = value[:, :mid]
            flip_ref[pl.ds(n * half + block * 8, 8)] = value[:, mid:]
    right = jnp.dot(flip_ref[...], fold_ref[...], precision=lax.Precision.HIGHEST, preferred_element_type=jnp.float32)
    for n, ref in enumerate((peak_ref, mean_ref, square_ref)):
        ref[0, :, mid:] = right[n * half:(n + 1) * half]


def flipped(x, axis, bits):
    return lax.ppermute(x, axis, [(i, i ^ bits) for i in range(lax.axis_size(axis))])


def crossed(x, even, odd):
    groups, orients, cores = (lax.axis_size(axis) for axis in ("groups", "orient", "tile"))
    pairs = []
    for g in range(groups):
        for o in range(orients):
            for c in range(cores):
                group_bits, orient_bits = odd if c else even
                pairs.append(((g * orients + o) * cores + c, ((g ^ group_bits) * orients + (o ^ orient_bits)) * cores + c))
    return lax.ppermute(x, ("groups", "orient", "tile"), pairs)


def shards(spectra, templates, weights):
    half, side = spectra.shape[2:]
    orients = lax.axis_size("orient")
    vmem = pl.BlockSpec(memory_space=pltpu.VMEM)
    hbm = pl.BlockSpec(memory_space=pltpu.HBM)
    params = pltpu.CompilerParams(vmem_limit_bytes=24 << 20)
    shape = lambda *dims, dtype=jnp.float32: jax.ShapeDtypeStruct(dims, dtype)
    scratch = lambda *dims: pltpu.VMEM(dims, jnp.float32)
    template = templates[0]

    coef, table, columns = pl.pallas_call(
        prepare_kernel,
        in_specs=[hbm] * 3,
        out_specs=[vmem] * 3,
        out_shape=[shape(4, half, side)] + [shape(2, side, side, dtype=jnp.bfloat16)] * 2,
        scratch_shapes=[
            scratch(2, half, side), scratch(half, side), scratch(side, side), scratch(side, side), pltpu.SemaphoreType.DMA((5,)),
        ],
        compiler_params=params,
        name="prepare",
    )(spectra[0], weights, jnp.asarray(np.stack([row_table(side, half), column_table(side)])))

    def maps(wholes, arrays=(), places=(), extra=8):
        return pl.pallas_call(
            functools.partial(maps_kernel, len(wholes), places),
            in_specs=[vmem] * (3 + len(wholes) + len(arrays)),
            out_specs=[vmem] * 2,
            out_shape=[shape(len(wholes) + len(places), half + extra, side)] * 2,
            compiler_params=params,
            name="maps",
        )(coef, table, columns, *wholes, *arrays)

    if lax.axis_size("groups") == 2 and orients == 8:
        plane = lax.axis_index("groups")
        few = 24
        pick = lambda whole, n: lax.dynamic_index_in_dim(whole, n, 0, keepdims=False)
        part = pick(template, plane)
        near1, near2 = (flipped(part, "orient", 2 * k) for k in (1, 2))
        beside = flipped(lax.optimization_barrier((template, part))[0], "orient", 1)
        near1, near2, beside = lax.optimization_barrier((near1, near2, beside))
        near = jnp.concatenate([near1, near2], 0)
        far = flipped(jnp.concatenate([near2, pick(beside, 1 - plane)], 0), "orient", 2)
        near_x = flipped(near, "groups", 1)
        near_y = flipped(near, "orient", 1)
        far, near_x, near_y, coef = lax.optimization_barrier((far, near_x, near_y, coef))
        last_y = flipped(jnp.concatenate([far[:half], near_x[half + few:]], 0), "orient", 1)
        last_x = flipped(jnp.concatenate([far[:half], near_y[half:half + few]], 0), "groups", 1)
        second = jnp.where(lax.axis_index("tile") == 0, near_x[half:], near_y[half:])
        corner = crossed(second, (0, 3), (1, 2))
        block = lambda array, start=0, rows=half: ((array, start, start + rows),)
        early = maps(
            [template, beside],
            [near, near_x, near_y, far],
            ((block(0), block(1)), (block(0, half), block(1, half)), (block(2), block(3, half))),
        )
        last_x, last_y, corner, early = lax.optimization_barrier((last_x, last_y, corner, early))
        late = maps(
            [],
            [near_y, last_x, last_y, far, corner],
            (
                (block(0, half), block(1, half, few) + block(2, half, half - few)),
                (block(3), block(1)),
                (block(2), block(4)),
            ),
        )
        calls = [early, late]
    else:
        rest = [template] + [flipped(template, "orient", k) for k in range(1, orients)]
        calls = [maps(rest[i:i + 4]) for i in range(0, len(rest), 4)]
    keeps = [keep for keep, _ in calls]
    recvs = [flipped(send, "tile", 1) for _, send in calls]
    return tuple(pl.pallas_call(
        functools.partial(stats_kernel, len(keeps), 2 * side * side),
        in_specs=[vmem] * (2 * len(keeps) + 1),
        out_specs=[vmem] * 3,
        out_shape=[shape(1, half, side)] * 3,
        scratch_shapes=[scratch(3 * half, side // 2)],
        compiler_params=params,
        name="statistics",
    )(*keeps, *recvs, jnp.asarray(unfold_table(side // 2))))


def solution(mesh):
    in_specs = (
        P(("groups", "orient"), None, "tile", None),
        P("orient", None, "tile", None),
        P("groups", None),
    )
    out_specs = (P(("groups", "orient"), "tile", None),) * 3
    return jax.shard_map(shards, mesh=mesh, in_specs=in_specs, out_specs=out_specs, check_vma=False)
```

```python
import functools
import math

import jax
import jax.numpy as jnp
import numpy as np
from jax import lax
from jax.experimental import pallas as pl
from jax.experimental.pallas import tpu as pltpu
from jax.sharding import PartitionSpec as P


def column_table(side):
    mid = side // 2
    k = np.arange(side)[:, None]
    x = np.arange(mid)[None, :]
    angle = 2.0 * math.pi * (k * x % side) / side
    right = np.sin(angle)
    right[:, 0] = np.cos(math.pi * k[:, 0])
    return np.concatenate([np.cos(angle), right], 1).astype(np.float32)


def row_table(side, half):
    y = np.arange(side)[:, None]
    k = np.arange(half)[None, :]
    angle = 2.0 * math.pi * (k * y % side) / side
    return np.concatenate([np.cos(angle), -np.sin(angle)], 1).astype(np.float32)


def unfold_table(mid):
    table = np.zeros((mid, mid), np.float32)
    k = np.arange(mid)
    table[(mid - k) % mid, k] = 1.0
    return table


def parts(x):
    high = x.astype(jnp.bfloat16)
    low = (x - high.astype(jnp.float32)).astype(jnp.bfloat16)
    return high, low


def dot(a, b):
    return jnp.dot(a, b, preferred_element_type=jnp.float32)


def prepare_kernel(s_hbm, w_hbm, table_hbm, coef_ref, rt_ref, ct_ref, s_ref, w_ref, row_ref, col_ref, sems):
    half, side = w_ref.shape
    here = lax.axis_index("tile")
    swap = lax.axis_index("groups") % 2
    mine = pl.ds(pl.multiple_of(here * half, half), half)
    other = pl.ds(pl.multiple_of((1 - here) * half, half), half)
    moves = (
        (s_hbm, s_ref),
        (w_hbm.at[mine], w_ref),
        (table_hbm.at[0, mine], row_ref.at[pl.ds(0, half)]),
        (table_hbm.at[0, other], row_ref.at[pl.ds(half, half)]),
        (table_hbm.at[1], col_ref),
    )
    copies = [pltpu.make_async_copy(source, target, sems.at[n]) for n, (source, target) in enumerate(moves)]
    for copy in copies:
        copy.start()
    for copy in copies:
        copy.wait()
    w = w_ref[...]
    u, v = s_ref[swap] * w, s_ref[1 - swap] * w
    turn = (1 - 2 * swap).astype(jnp.float32)
    coef_ref[0], coef_ref[1], coef_ref[2], coef_ref[3] = u, v, u * turn, v * turn
    ct_ref[0], ct_ref[1] = parts(col_ref[...])
    odd = lax.broadcasted_iota(jnp.int32, (side, side), 0) % 2
    rt_ref[0], rt_ref[1] = parts(row_ref[...] * (1 - 2 * odd * here).astype(jnp.float32))


def correlate(a, b, coef_ref, col_ref, rt_ref, keep_ref, send_ref, n):
    half, side = a.shape
    mid = side // 2
    squares = jnp.sum((a * a + b * b).reshape(half // 8, 8, side), axis=0)
    power = jnp.broadcast_to(jnp.sum(squares), (keep_ref.shape[1] - half, side))
    z = jnp.concatenate([coef_ref[0] * a + coef_ref[1] * b, coef_ref[3] * a - coef_ref[2] * b], 0)
    zh, zl = parts(z)
    ch, cl = col_ref[0], col_ref[1]
    m = dot(zh, ch) + (dot(zl, ch) + dot(zh, cl))
    mcr, mci = m[:half, :mid], m[half:, :mid]
    msr, msi = m[:half, mid:], m[half:, mid:]
    first = lax.broadcasted_iota(jnp.int32, (half, mid), 1) == 0
    real = jnp.concatenate([mcr - jnp.where(first, 0.0, msi), jnp.where(first, msr, mcr + msi)], 1)
    imag = jnp.concatenate([mci + jnp.where(first, 0.0, msr), jnp.where(first, msi, mci - msr)], 1)
    ah, al = parts(jnp.concatenate([real, imag], 0))
    rh, rl = rt_ref[0], rt_ref[1]
    p = dot(rh, ah) + (dot(rh, al) + dot(rl, ah))
    keep_ref[n, :half] = p[:half]
    keep_ref[n, half:] = power
    send_ref[n, :half] = p[half:]
    send_ref[n, half:] = power


def maps_kernel(wholes, places, coef_ref, rt_ref, col_ref, *refs):
    inputs, (keep_ref, send_ref) = refs[:-2], refs[-2:]
    whole_refs, part_refs = inputs[:wholes], inputs[wholes:]
    swap = lax.axis_index("groups") % 2
    for n, ref in enumerate(whole_refs):
        correlate(ref[swap], ref[1 - swap], coef_ref, col_ref, rt_ref, keep_ref, send_ref, n)
    for n, pair in enumerate(places):
        a, b = (jnp.concatenate([part_refs[array][start:stop] for array, start, stop in pieces], 0) for pieces in pair)
        correlate(a, b, coef_ref, col_ref, rt_ref, keep_ref, send_ref, wholes + n)


def stats_kernel(calls, entries, *refs):
    keeps, recvs = refs[:calls], refs[calls:2 * calls]
    fold_ref, peak_ref, mean_ref, square_ref, flip_ref = refs[2 * calls:]
    half, side = peak_ref.shape[1:]
    mid = side // 2
    pairs = [(keep, recv, n) for keep, recv in zip(keeps, recvs) for n in range(keep.shape[0])]
    count = len(pairs)
    for block in range(half // 8):
        rows = pl.ds(block * 8, 8)
        best = total = squares = None
        for keep, recv, n in pairs:
            power = (keep[n, half:half + 8] + recv[n, half:half + 8]) * (1.0 / entries)
            scale = lax.rsqrt(power + 1e-6) * (1.0 / side)
            c = (keep[n, rows] + recv[n, rows]) * scale
            if best is None:
                best, total, squares = c, c, c * c
            else:
                best, total, squares = jnp.maximum(best, c), total + c, squares + c * c
        total = total * (1.0 / count)
        squares = squares * (1.0 / count)
        for n, (ref, value) in enumerate(((peak_ref, best), (mean_ref, total), (square_ref, squares))):
            ref[0, rows, :mid] = value[:, :mid]
            flip_ref[pl.ds(n * half + block * 8, 8)] = value[:, mid:]
    right = jnp.dot(flip_ref[...], fold_ref[...], precision=lax.Precision.HIGHEST, preferred_element_type=jnp.float32)
    for n, ref in enumerate((peak_ref, mean_ref, square_ref)):
        ref[0, :, mid:] = right[n * half:(n + 1) * half]


def flipped(x, axis, bits):
    return lax.ppermute(x, axis, [(i, i ^ bits) for i in range(lax.axis_size(axis))])


def crossed(x, even, odd):
    groups, orients, cores = (lax.axis_size(axis) for axis in ("groups", "orient", "tile"))
    pairs = []
    for g in range(groups):
        for o in range(orients):
            for c in range(cores):
                group_bits, orient_bits = odd if c else even
                pairs.append(((g * orients + o) * cores + c, ((g ^ group_bits) * orients + (o ^ orient_bits)) * cores + c))
    return lax.ppermute(x, ("groups", "orient", "tile"), pairs)


def shards(spectra, templates, weights):
    half, side = spectra.shape[2:]
    orients = lax.axis_size("orient")
    vmem = pl.BlockSpec(memory_space=pltpu.VMEM)
    hbm = pl.BlockSpec(memory_space=pltpu.HBM)
    params = pltpu.CompilerParams(vmem_limit_bytes=24 << 20)
    shape = lambda *dims, dtype=jnp.float32: jax.ShapeDtypeStruct(dims, dtype)
    scratch = lambda *dims: pltpu.VMEM(dims, jnp.float32)
    template = templates[0]

    coef, table, columns = pl.pallas_call(
        prepare_kernel,
        in_specs=[hbm] * 3,
        out_specs=[vmem] * 3,
        out_shape=[shape(4, half, side)] + [shape(2, side, side, dtype=jnp.bfloat16)] * 2,
        scratch_shapes=[
            scratch(2, half, side), scratch(half, side), scratch(side, side), scratch(side, side), pltpu.SemaphoreType.DMA((5,)),
        ],
        compiler_params=params,
        name="prepare",
    )(spectra[0], weights, jnp.asarray(np.stack([row_table(side, half), column_table(side)])))

    def maps(wholes, arrays=(), places=(), extra=8):
        return pl.pallas_call(
            functools.partial(maps_kernel, len(wholes), places),
            in_specs=[vmem] * (3 + len(wholes) + len(arrays)),
            out_specs=[vmem] * 2,
            out_shape=[shape(len(wholes) + len(places), half + extra, side)] * 2,
            compiler_params=params,
            name="maps",
        )(coef, table, columns, *wholes, *arrays)

    if lax.axis_size("groups") == 2 and orients == 8:
        plane = lax.axis_index("groups")
        few = 104
        pick = lambda whole, n: lax.dynamic_index_in_dim(whole, n, 0, keepdims=False)
        part = pick(template, plane)
        near1, near2 = (flipped(part, "orient", 2 * k) for k in (1, 2))
        beside = flipped(lax.optimization_barrier((template, part))[0], "orient", 1)
        near1, near2, beside = lax.optimization_barrier((near1, near2, beside))
        near = jnp.concatenate([near1, near2], 0)
        far = flipped(jnp.concatenate([near2, pick(beside, 1 - plane)], 0), "orient", 2)
        near_x = flipped(near, "groups", 1)
        near_y = flipped(near, "orient", 1)
        far, near_x, near_y, coef = lax.optimization_barrier((far, near_x, near_y, coef))
        last_y = flipped(jnp.concatenate([far[:half], near_x[half + few:]], 0), "orient", 1)
        last_x = flipped(jnp.concatenate([far[:half], near_y[half:half + few]], 0), "groups", 1)
        second = jnp.where(lax.axis_index("tile") == 0, near_x[half:], near_y[half:])
        corner = crossed(second, (0, 3), (1, 2))
        block = lambda array, start=0, rows=half: ((array, start, start + rows),)
        early = maps(
            [template, beside],
            [near, near_x, near_y, far],
            ((block(0), block(1)), (block(0, half), block(1, half)), (block(2), block(3, half))),
        )
        last_x, last_y, corner, early = lax.optimization_barrier((last_x, last_y, corner, early))
        late = maps(
            [],
            [near_y, last_x, last_y, far, corner],
            (
                (block(0, half), block(1, half, few) + block(2, half, half - few)),
                (block(3), block(1)),
                (block(2), block(4)),
            ),
        )
        calls = [early, late]
    else:
        rest = [template] + [flipped(template, "orient", k) for k in range(1, orients)]
        calls = [maps(rest[i:i + 4]) for i in range(0, len(rest), 4)]
    keeps = [keep for keep, _ in calls]
    recvs = [flipped(send, "tile", 1) for _, send in calls]
    return tuple(pl.pallas_call(
        functools.partial(stats_kernel, len(keeps), 2 * side * side),
        in_specs=[vmem] * (2 * len(keeps) + 1),
        out_specs=[vmem] * 3,
        out_shape=[shape(1, half, side)] * 3,
        scratch_shapes=[scratch(3 * half, side // 2)],
        compiler_params=params,
        name="statistics",
    )(*keeps, *recvs, jnp.asarray(unfold_table(side // 2))))


def solution(mesh):
    in_specs = (
        P(("groups", "orient"), None, "tile", None),
        P("orient", None, "tile", None),
        P("groups", None),
    )
    out_specs = (P(("groups", "orient"), "tile", None),) * 3
    return jax.shard_map(shards, mesh=mesh, in_specs=in_specs, out_specs=out_specs, check_vma=False)
```

```python
import functools
import math

import jax
import jax.numpy as jnp
import numpy as np
from jax import lax
from jax.experimental import pallas as pl
from jax.experimental.pallas import tpu as pltpu
from jax.sharding import PartitionSpec as P


def column_table(side):
    mid = side // 2
    k = np.arange(side)[:, None]
    x = np.arange(mid)[None, :]
    angle = 2.0 * math.pi * (k * x % side) / side
    right = np.sin(angle)
    right[:, 0] = np.cos(math.pi * k[:, 0])
    return np.concatenate([np.cos(angle), right], 1).astype(np.float32)


def row_table(side, half):
    y = np.arange(side)[:, None]
    k = np.arange(half)[None, :]
    angle = 2.0 * math.pi * (k * y % side) / side
    return np.concatenate([np.cos(angle), -np.sin(angle)], 1).astype(np.float32)


def unfold_table(mid):
    table = np.zeros((mid, mid), np.float32)
    k = np.arange(mid)
    table[(mid - k) % mid, k] = 1.0
    return table


def parts(x):
    high = x.astype(jnp.bfloat16)
    low = (x - high.astype(jnp.float32)).astype(jnp.bfloat16)
    return high, low


def dot(a, b):
    return jnp.dot(a, b, preferred_element_type=jnp.float32)


def prepare_kernel(s_hbm, w_hbm, table_hbm, coef_ref, rt_ref, ct_ref, s_ref, w_ref, row_ref, col_ref, sems):
    half, side = w_ref.shape
    here = lax.axis_index("tile")
    swap = lax.axis_index("groups") % 2
    mine = pl.ds(pl.multiple_of(here * half, half), half)
    other = pl.ds(pl.multiple_of((1 - here) * half, half), half)
    moves = (
        (s_hbm, s_ref),
        (w_hbm.at[mine], w_ref),
        (table_hbm.at[0, mine], row_ref.at[pl.ds(0, half)]),
        (table_hbm.at[0, other], row_ref.at[pl.ds(half, half)]),
        (table_hbm.at[1], col_ref),
    )
    copies = [pltpu.make_async_copy(source, target, sems.at[n]) for n, (source, target) in enumerate(moves)]
    for copy in copies:
        copy.start()
    for copy in copies:
        copy.wait()
    w = w_ref[...]
    u, v = s_ref[swap] * w, s_ref[1 - swap] * w
    turn = (1 - 2 * swap).astype(jnp.float32)
    coef_ref[0], coef_ref[1], coef_ref[2], coef_ref[3] = u, v, u * turn, v * turn
    ct_ref[0], ct_ref[1] = parts(col_ref[...])
    odd = lax.broadcasted_iota(jnp.int32, (side, side), 0) % 2
    rt_ref[0], rt_ref[1] = parts(row_ref[...] * (1 - 2 * odd * here).astype(jnp.float32))


def correlate(a, b, coef_ref, col_ref, rt_ref, keep_ref, send_ref, n):
    half, side = a.shape
    mid = side // 2
    squares = jnp.sum((a * a + b * b).reshape(half // 8, 8, side), axis=0)
    power = jnp.broadcast_to(jnp.sum(squares), (keep_ref.shape[1] - half, side))
    z = jnp.concatenate([coef_ref[0] * a + coef_ref[1] * b, coef_ref[3] * a - coef_ref[2] * b], 0)
    zh, zl = parts(z)
    ch, cl = col_ref[0], col_ref[1]
    m = dot(zh, ch) + (dot(zl, ch) + dot(zh, cl))
    mcr, mci = m[:half, :mid], m[half:, :mid]
    msr, msi = m[:half, mid:], m[half:, mid:]
    first = lax.broadcasted_iota(jnp.int32, (half, mid), 1) == 0
    real = jnp.concatenate([mcr - jnp.where(first, 0.0, msi), jnp.where(first, msr, mcr + msi)], 1)
    imag = jnp.concatenate([mci + jnp.where(first, 0.0, msr), jnp.where(first, msi, mci - msr)], 1)
    ah, al = parts(jnp.concatenate([real, imag], 0))
    rh, rl = rt_ref[0], rt_ref[1]
    p = dot(rh, ah) + (dot(rh, al) + dot(rl, ah))
    keep_ref[n, :half] = p[:half]
    keep_ref[n, half:] = power
    send_ref[n, :half] = p[half:]
    send_ref[n, half:] = power


def maps_kernel(wholes, places, coef_ref, rt_ref, col_ref, *refs):
    inputs, (keep_ref, send_ref) = refs[:-2], refs[-2:]
    whole_refs, part_refs = inputs[:wholes], inputs[wholes:]
    swap = lax.axis_index("groups") % 2
    for n, ref in enumerate(whole_refs):
        correlate(ref[swap], ref[1 - swap], coef_ref, col_ref, rt_ref, keep_ref, send_ref, n)
    for n, pair in enumerate(places):
        a, b = (jnp.concatenate([part_refs[array][start:stop] for array, start, stop in pieces], 0) for pieces in pair)
        correlate(a, b, coef_ref, col_ref, rt_ref, keep_ref, send_ref, wholes + n)


def stats_kernel(calls, entries, *refs):
    keeps, recvs = refs[:calls], refs[calls:2 * calls]
    fold_ref, peak_ref, mean_ref, square_ref, flip_ref = refs[2 * calls:]
    half, side = peak_ref.shape[1:]
    mid = side // 2
    pairs = [(keep, recv, n) for keep, recv in zip(keeps, recvs) for n in range(keep.shape[0])]
    count = len(pairs)
    scales = []
    for keep, recv, n in pairs:
        power = (keep[n, half:half + 8] + recv[n, half:half + 8]) * (1.0 / entries)
        scales.append(lax.rsqrt(power + 1e-6) * (1.0 / side))

    def block(i, carry):
        start = pl.multiple_of(i * 8, 8)
        rows = pl.ds(start, 8)
        best = total = squares = None
        for (keep, recv, n), scale in zip(pairs, scales):
            c = (keep[n, rows] + recv[n, rows]) * scale
            if best is None:
                best, total, squares = c, c, c * c
            else:
                best, total, squares = jnp.maximum(best, c), total + c, squares + c * c
        total = total * (1.0 / count)
        squares = squares * (1.0 / count)
        for n, (ref, value) in enumerate(((peak_ref, best), (mean_ref, total), (square_ref, squares))):
            ref[0, rows, :mid] = value[:, :mid]
            flip_ref[pl.ds(pl.multiple_of(n * half + start, 8), 8)] = value[:, mid:]
        return carry

    lax.fori_loop(0, half // 8, block, 0, unroll=2)
    right = jnp.dot(flip_ref[...], fold_ref[...], precision=lax.Precision.HIGHEST, preferred_element_type=jnp.float32)
    for n, ref in enumerate((peak_ref, mean_ref, square_ref)):
        ref[0, :, mid:] = right[n * half:(n + 1) * half]


def flipped(x, axis, bits):
    return lax.ppermute(x, axis, [(i, i ^ bits) for i in range(lax.axis_size(axis))])


def crossed(x, even, odd):
    groups, orients, cores = (lax.axis_size(axis) for axis in ("groups", "orient", "tile"))
    pairs = []
    for g in range(groups):
        for o in range(orients):
            for c in range(cores):
                group_bits, orient_bits = odd if c else even
                pairs.append(((g * orients + o) * cores + c, ((g ^ group_bits) * orients + (o ^ orient_bits)) * cores + c))
    return lax.ppermute(x, ("groups", "orient", "tile"), pairs)


def shards(spectra, templates, weights):
    half, side = spectra.shape[2:]
    orients = lax.axis_size("orient")
    vmem = pl.BlockSpec(memory_space=pltpu.VMEM)
    hbm = pl.BlockSpec(memory_space=pltpu.HBM)
    params = pltpu.CompilerParams(vmem_limit_bytes=24 << 20)
    shape = lambda *dims, dtype=jnp.float32: jax.ShapeDtypeStruct(dims, dtype)
    scratch = lambda *dims: pltpu.VMEM(dims, jnp.float32)
    template = templates[0]

    coef, table, columns = pl.pallas_call(
        prepare_kernel,
        in_specs=[hbm] * 3,
        out_specs=[vmem] * 3,
        out_shape=[shape(4, half, side)] + [shape(2, side, side, dtype=jnp.bfloat16)] * 2,
        scratch_shapes=[
            scratch(2, half, side), scratch(half, side), scratch(side, side), scratch(side, side), pltpu.SemaphoreType.DMA((5,)),
        ],
        compiler_params=params,
        name="prepare",
    )(spectra[0], weights, jnp.asarray(np.stack([row_table(side, half), column_table(side)])))

    def maps(wholes, arrays=(), places=(), extra=8):
        return pl.pallas_call(
            functools.partial(maps_kernel, len(wholes), places),
            in_specs=[vmem] * (3 + len(wholes) + len(arrays)),
            out_specs=[vmem] * 2,
            out_shape=[shape(len(wholes) + len(places), half + extra, side)] * 2,
            compiler_params=params,
            name="maps",
        )(coef, table, columns, *wholes, *arrays)

    if lax.axis_size("groups") == 2 and orients == 8:
        plane = lax.axis_index("groups")
        few = 56
        pick = lambda whole, n: lax.dynamic_index_in_dim(whole, n, 0, keepdims=False)
        part = pick(template, plane)
        near1, near2 = (flipped(part, "orient", 2 * k) for k in (1, 2))
        beside = flipped(lax.optimization_barrier((template, part))[0], "orient", 1)
        near1, near2, beside = lax.optimization_barrier((near1, near2, beside))
        near = jnp.concatenate([near1, near2], 0)
        far = flipped(jnp.concatenate([near2, pick(beside, 1 - plane)], 0), "orient", 2)
        near_x = flipped(near, "groups", 1)
        near_y = flipped(near, "orient", 1)
        far, near_x, near_y, coef = lax.optimization_barrier((far, near_x, near_y, coef))
        last_y = flipped(jnp.concatenate([far[:half], near_x[half + few:]], 0), "orient", 1)
        last_x = flipped(jnp.concatenate([far[:half], near_y[half:half + few]], 0), "groups", 1)
        second = jnp.where(lax.axis_index("tile") == 0, near_x[half:], near_y[half:])
        corner = crossed(second, (0, 3), (1, 2))
        block = lambda array, start=0, rows=half: ((array, start, start + rows),)
        early = maps(
            [template, beside],
            [near, near_x, near_y, far],
            ((block(0), block(1)), (block(0, half), block(1, half)), (block(2), block(3, half))),
        )
        last_x, last_y, corner, early = lax.optimization_barrier((last_x, last_y, corner, early))
        late = maps(
            [],
            [near_y, last_x, last_y, far, corner],
            (
                (block(0, half), block(1, half, few) + block(2, half, half - few)),
                (block(3), block(1)),
                (block(2), block(4)),
            ),
        )
        calls = [early, late]
    else:
        rest = [template] + [flipped(template, "orient", k) for k in range(1, orients)]
        calls = [maps(rest[i:i + 4]) for i in range(0, len(rest), 4)]
    keeps = [keep for keep, _ in calls]
    recvs = [flipped(send, "tile", 1) for _, send in calls]
    return tuple(pl.pallas_call(
        functools.partial(stats_kernel, len(keeps), 2 * side * side),
        in_specs=[vmem] * (2 * len(keeps) + 1),
        out_specs=[vmem] * 3,
        out_shape=[shape(1, half, side)] * 3,
        scratch_shapes=[scratch(3 * half, side // 2)],
        compiler_params=params,
        name="statistics",
    )(*keeps, *recvs, jnp.asarray(unfold_table(side // 2))))


def solution(mesh):
    in_specs = (
        P(("groups", "orient"), None, "tile", None),
        P("orient", None, "tile", None),
        P("groups", None),
    )
    out_specs = (P(("groups", "orient"), "tile", None),) * 3
    return jax.shard_map(shards, mesh=mesh, in_specs=in_specs, out_specs=out_specs, check_vma=False)
```

```python
import functools
import math

import jax
import jax.numpy as jnp
import numpy as np
from jax import lax
from jax.experimental import pallas as pl
from jax.experimental.pallas import tpu as pltpu
from jax.sharding import PartitionSpec as P


def column_table(side):
    mid = side // 2
    k = np.arange(side)[:, None]
    x = np.arange(mid)[None, :]
    angle = 2.0 * math.pi * (k * x % side) / side
    right = np.sin(angle)
    right[:, 0] = np.cos(math.pi * k[:, 0])
    return np.concatenate([np.cos(angle), right], 1).astype(np.float32)


def row_table(side, half):
    y = np.arange(side)[:, None]
    k = np.arange(half)[None, :]
    angle = 2.0 * math.pi * (k * y % side) / side
    return np.concatenate([np.cos(angle), -np.sin(angle)], 1).astype(np.float32)


def unfold_table(mid):
    table = np.zeros((mid, mid), np.float32)
    k = np.arange(mid)
    table[(mid - k) % mid, k] = 1.0
    return table


def parts(x):
    high = x.astype(jnp.bfloat16)
    low = (x - high.astype(jnp.float32)).astype(jnp.bfloat16)
    return high, low


def dot(a, b):
    return jnp.dot(a, b, preferred_element_type=jnp.float32)


def prepare_kernel(s_hbm, w_hbm, table_hbm, coef_ref, rt_ref, ct_ref, s_ref, w_ref, row_ref, col_ref, sems):
    half, side = w_ref.shape
    here = lax.axis_index("tile")
    swap = lax.axis_index("groups") % 2
    mine = pl.ds(pl.multiple_of(here * half, half), half)
    other = pl.ds(pl.multiple_of((1 - here) * half, half), half)
    moves = (
        (s_hbm, s_ref),
        (w_hbm.at[mine], w_ref),
        (table_hbm.at[0, mine], row_ref.at[pl.ds(0, half)]),
        (table_hbm.at[0, other], row_ref.at[pl.ds(half, half)]),
        (table_hbm.at[1], col_ref),
    )
    copies = [pltpu.make_async_copy(source, target, sems.at[n]) for n, (source, target) in enumerate(moves)]
    for copy in copies:
        copy.start()
    for copy in copies:
        copy.wait()
    w = w_ref[...]
    u, v = s_ref[swap] * w, s_ref[1 - swap] * w
    turn = (1 - 2 * swap).astype(jnp.float32)
    coef_ref[0], coef_ref[1], coef_ref[2], coef_ref[3] = u, v, u * turn, v * turn
    ct_ref[0], ct_ref[1] = parts(col_ref[...])
    odd = lax.broadcasted_iota(jnp.int32, (side, side), 0) % 2
    rt_ref[0], rt_ref[1] = parts(row_ref[...] * (1 - 2 * odd * here).astype(jnp.float32))


def correlate(a, b, coef_ref, col_ref, rt_ref, keep_ref, send_ref, n):
    half, side = a.shape
    mid = side // 2
    squares = jnp.sum((a * a + b * b).reshape(half // 8, 8, side), axis=0)
    power = jnp.broadcast_to(jnp.sum(squares), (keep_ref.shape[1] - half, side))
    z = jnp.concatenate([coef_ref[0] * a + coef_ref[1] * b, coef_ref[3] * a - coef_ref[2] * b], 0)
    zh, zl = parts(z)
    ch, cl = col_ref[0], col_ref[1]
    m = dot(zh, ch) + (dot(zl, ch) + dot(zh, cl))
    mcr, mci = m[:half, :mid], m[half:, :mid]
    msr, msi = m[:half, mid:], m[half:, mid:]
    first = lax.broadcasted_iota(jnp.int32, (half, mid), 1) == 0
    real = jnp.concatenate([mcr - jnp.where(first, 0.0, msi), jnp.where(first, msr, mcr + msi)], 1)
    imag = jnp.concatenate([mci + jnp.where(first, 0.0, msr), jnp.where(first, msi, mci - msr)], 1)
    ah, al = parts(jnp.concatenate([real, imag], 0))
    rh, rl = rt_ref[0], rt_ref[1]
    p = dot(rh, ah) + (dot(rh, al) + dot(rl, ah))
    keep_ref[n, :half] = p[:half]
    keep_ref[n, half:] = power
    send_ref[n, :half] = p[half:]
    send_ref[n, half:] = power


def maps_kernel(wholes, places, coef_ref, rt_ref, col_ref, *refs):
    inputs, (keep_ref, send_ref) = refs[:-2], refs[-2:]
    whole_refs, part_refs = inputs[:wholes], inputs[wholes:]
    swap = lax.axis_index("groups") % 2
    for n, ref in enumerate(whole_refs):
        correlate(ref[swap], ref[1 - swap], coef_ref, col_ref, rt_ref, keep_ref, send_ref, n)
    for n, pair in enumerate(places):
        a, b = (jnp.concatenate([part_refs[array][start:stop] for array, start, stop in pieces], 0) for pieces in pair)
        correlate(a, b, coef_ref, col_ref, rt_ref, keep_ref, send_ref, wholes + n)


def stats_kernel(calls, entries, *refs):
    keeps, recvs = refs[:calls], refs[calls:2 * calls]
    fold_ref, peak_ref, mean_ref, square_ref, flip_ref = refs[2 * calls:]
    half, side = peak_ref.shape[1:]
    mid = side // 2
    pairs = [(keep, recv, n) for keep, recv in zip(keeps, recvs) for n in range(keep.shape[0])]
    count = len(pairs)
    for block in range(half // 8):
        rows = pl.ds(block * 8, 8)
        best = total = squares = None
        for keep, recv, n in pairs:
            power = (keep[n, half:half + 8] + recv[n, half:half + 8]) * (1.0 / entries)
            scale = lax.rsqrt(power + 1e-6) * (1.0 / side)
            c = (keep[n, rows] + recv[n, rows]) * scale
            if best is None:
                best, total, squares = c, c, c * c
            else:
                best, total, squares = jnp.maximum(best, c), total + c, squares + c * c
        total = total * (1.0 / count)
        squares = squares * (1.0 / count)
        for n, (ref, value) in enumerate(((peak_ref, best), (mean_ref, total), (square_ref, squares))):
            ref[0, rows, :mid] = value[:, :mid]
            flip_ref[pl.ds(n * half + block * 8, 8)] = value[:, mid:]
    right = jnp.dot(flip_ref[...], fold_ref[...], precision=lax.Precision.HIGHEST, preferred_element_type=jnp.float32)
    for n, ref in enumerate((peak_ref, mean_ref, square_ref)):
        ref[0, :, mid:] = right[n * half:(n + 1) * half]


def flipped(x, axis, bits):
    return lax.ppermute(x, axis, [(i, i ^ bits) for i in range(lax.axis_size(axis))])


def crossed(x, even, odd):
    groups, orients, cores = (lax.axis_size(axis) for axis in ("groups", "orient", "tile"))
    pairs = []
    for g in range(groups):
        for o in range(orients):
            for c in range(cores):
                group_bits, orient_bits = odd if c else even
                pairs.append(((g * orients + o) * cores + c, ((g ^ group_bits) * orients + (o ^ orient_bits)) * cores + c))
    return lax.ppermute(x, ("groups", "orient", "tile"), pairs)


def shards(spectra, templates, weights):
    half, side = spectra.shape[2:]
    orients = lax.axis_size("orient")
    vmem = pl.BlockSpec(memory_space=pltpu.VMEM)
    hbm = pl.BlockSpec(memory_space=pltpu.HBM)
    params = pltpu.CompilerParams(vmem_limit_bytes=24 << 20)
    shape = lambda *dims, dtype=jnp.float32: jax.ShapeDtypeStruct(dims, dtype)
    scratch = lambda *dims: pltpu.VMEM(dims, jnp.float32)
    template = templates[0]

    coef, table, columns = pl.pallas_call(
        prepare_kernel,
        in_specs=[hbm] * 3,
        out_specs=[vmem] * 3,
        out_shape=[shape(4, half, side)] + [shape(2, side, side, dtype=jnp.bfloat16)] * 2,
        scratch_shapes=[
            scratch(2, half, side), scratch(half, side), scratch(side, side), scratch(side, side), pltpu.SemaphoreType.DMA((5,)),
        ],
        compiler_params=params,
        name="prepare",
    )(spectra[0], weights, jnp.asarray(np.stack([row_table(side, half), column_table(side)])))

    def maps(wholes, arrays=(), places=(), extra=8):
        return pl.pallas_call(
            functools.partial(maps_kernel, len(wholes), places),
            in_specs=[vmem] * (3 + len(wholes) + len(arrays)),
            out_specs=[vmem] * 2,
            out_shape=[shape(len(wholes) + len(places), half + extra, side)] * 2,
            compiler_params=params,
            name="maps",
        )(coef, table, columns, *wholes, *arrays)

    if lax.axis_size("groups") == 2 and orients == 8:
        plane = lax.axis_index("groups")
        few = 72
        pick = lambda whole, n: lax.dynamic_index_in_dim(whole, n, 0, keepdims=False)
        part = pick(template, plane)
        near1, near2 = (flipped(part, "orient", 2 * k) for k in (1, 2))
        beside = flipped(lax.optimization_barrier((template, part))[0], "orient", 1)
        near1, near2, beside = lax.optimization_barrier((near1, near2, beside))
        near = jnp.concatenate([near1, near2], 0)
        far = flipped(jnp.concatenate([near2, pick(beside, 1 - plane)], 0), "orient", 2)
        near_x = flipped(near, "groups", 1)
        near_y = flipped(near, "orient", 1)
        far, near_x, near_y, coef = lax.optimization_barrier((far, near_x, near_y, coef))
        last_y = flipped(jnp.concatenate([far[:half], near_x[half + few:]], 0), "orient", 1)
        last_x = flipped(jnp.concatenate([far[:half], near_y[half:half + few]], 0), "groups", 1)
        corner = crossed(near_y[half:], (1, 2), (1, 2))
        block = lambda array, start=0, rows=half: ((array, start, start + rows),)
        early = maps(
            [template, beside],
            [near, near_x, near_y, far],
            ((block(0), block(1)), (block(0, half), block(1, half)), (block(2), block(3, half))),
        )
        last_x, last_y, corner, early = lax.optimization_barrier((last_x, last_y, corner, early))
        late = maps(
            [],
            [near_y, last_x, last_y, far, corner],
            (
                (block(0, half), block(1, half, few) + block(2, half, half - few)),
                (block(3), block(1)),
                (block(2), block(4)),
            ),
        )
        calls = [early, late]
    else:
        rest = [template] + [flipped(template, "orient", k) for k in range(1, orients)]
        calls = [maps(rest[i:i + 4]) for i in range(0, len(rest), 4)]
    keeps = [keep for keep, _ in calls]
    recvs = [flipped(send, "tile", 1) for _, send in calls]
    return tuple(pl.pallas_call(
        functools.partial(stats_kernel, len(keeps), 2 * side * side),
        in_specs=[vmem] * (2 * len(keeps) + 1),
        out_specs=[vmem] * 3,
        out_shape=[shape(1, half, side)] * 3,
        scratch_shapes=[scratch(3 * half, side // 2)],
        compiler_params=params,
        name="statistics",
    )(*keeps, *recvs, jnp.asarray(unfold_table(side // 2))))


def solution(mesh):
    in_specs = (
        P(("groups", "orient"), None, "tile", None),
        P("orient", None, "tile", None),
        P("groups", None),
    )
    out_specs = (P(("groups", "orient"), "tile", None),) * 3
    return jax.shard_map(shards, mesh=mesh, in_specs=in_specs, out_specs=out_specs, check_vma=False)
```

```python
import functools
import math

import jax
import jax.numpy as jnp
import numpy as np
from jax import lax
from jax.experimental import pallas as pl
from jax.experimental.pallas import tpu as pltpu
from jax.sharding import PartitionSpec as P


def column_table(side):
    mid = side // 2
    k = np.arange(side)[:, None]
    x = np.arange(mid)[None, :]
    angle = 2.0 * math.pi * (k * x % side) / side
    right = np.sin(angle)
    right[:, 0] = np.cos(math.pi * k[:, 0])
    return np.concatenate([np.cos(angle), right], 1).astype(np.float32)


def row_table(side, half):
    y = np.arange(side)[:, None]
    k = np.arange(half)[None, :]
    angle = 2.0 * math.pi * (k * y % side) / side
    return np.concatenate([np.cos(angle), -np.sin(angle)], 1).astype(np.float32)


def unfold_table(mid):
    table = np.zeros((mid, mid), np.float32)
    k = np.arange(mid)
    table[(mid - k) % mid, k] = 1.0
    return table


def parts(x):
    high = x.astype(jnp.bfloat16)
    low = (x - high.astype(jnp.float32)).astype(jnp.bfloat16)
    return high, low


def dot(a, b):
    return jnp.dot(a, b, preferred_element_type=jnp.float32)


def prepare_kernel(s_hbm, w_hbm, table_hbm, coef_ref, rt_ref, ct_ref, s_ref, w_ref, row_ref, col_ref, sems):
    half, side = w_ref.shape
    here = lax.axis_index("tile")
    swap = lax.axis_index("groups") % 2
    mine = pl.ds(pl.multiple_of(here * half, half), half)
    other = pl.ds(pl.multiple_of((1 - here) * half, half), half)
    moves = (
        (s_hbm, s_ref),
        (w_hbm.at[mine], w_ref),
        (table_hbm.at[0, mine], row_ref.at[pl.ds(0, half)]),
        (table_hbm.at[0, other], row_ref.at[pl.ds(half, half)]),
        (table_hbm.at[1], col_ref),
    )
    copies = [pltpu.make_async_copy(source, target, sems.at[n]) for n, (source, target) in enumerate(moves)]
    for copy in copies:
        copy.start()
    for copy in copies:
        copy.wait()
    w = w_ref[...]
    u, v = s_ref[swap] * w, s_ref[1 - swap] * w
    turn = (1 - 2 * swap).astype(jnp.float32)
    coef_ref[0], coef_ref[1], coef_ref[2], coef_ref[3] = u, v, u * turn, v * turn
    ct_ref[0], ct_ref[1] = parts(col_ref[...])
    odd = lax.broadcasted_iota(jnp.int32, (side, side), 0) % 2
    rt_ref[0], rt_ref[1] = parts(row_ref[...] * (1 - 2 * odd * here).astype(jnp.float32))


def correlate(a, b, coef_ref, col_ref, rt_ref, keep_ref, send_ref, n):
    half, side = a.shape
    mid = side // 2
    squares = jnp.sum((a * a + b * b).reshape(half // 8, 8, side), axis=0)
    power = jnp.broadcast_to(jnp.sum(squares), (keep_ref.shape[1] - half, side))
    z = jnp.concatenate([coef_ref[0] * a + coef_ref[1] * b, coef_ref[3] * a - coef_ref[2] * b], 0)
    zh, zl = parts(z)
    ch, cl = col_ref[0], col_ref[1]
    m = dot(jnp.concatenate([zh, zl, zh], 1), jnp.concatenate([ch, ch, cl], 0))
    mcr, mci = m[:half, :mid], m[half:, :mid]
    msr, msi = m[:half, mid:], m[half:, mid:]
    first = lax.broadcasted_iota(jnp.int32, (half, mid), 1) == 0
    real = jnp.concatenate([mcr - jnp.where(first, 0.0, msi), jnp.where(first, msr, mcr + msi)], 1)
    imag = jnp.concatenate([mci + jnp.where(first, 0.0, msr), jnp.where(first, msi, mci - msr)], 1)
    ah, al = parts(jnp.concatenate([real, imag], 0))
    rh, rl = rt_ref[0], rt_ref[1]
    p = dot(jnp.concatenate([rh, rh, rl], 1), jnp.concatenate([ah, al, ah], 0))
    keep_ref[n, :half] = p[:half]
    keep_ref[n, half:] = power
    send_ref[n, :half] = p[half:]
    send_ref[n, half:] = power


def maps_kernel(wholes, places, coef_ref, rt_ref, col_ref, *refs):
    inputs, (keep_ref, send_ref) = refs[:-2], refs[-2:]
    whole_refs, part_refs = inputs[:wholes], inputs[wholes:]
    swap = lax.axis_index("groups") % 2
    for n, ref in enumerate(whole_refs):
        correlate(ref[swap], ref[1 - swap], coef_ref, col_ref, rt_ref, keep_ref, send_ref, n)
    for n, pair in enumerate(places):
        a, b = (jnp.concatenate([part_refs[array][start:stop] for array, start, stop in pieces], 0) for pieces in pair)
        correlate(a, b, coef_ref, col_ref, rt_ref, keep_ref, send_ref, wholes + n)


def stats_kernel(calls, entries, *refs):
    keeps, recvs = refs[:calls], refs[calls:2 * calls]
    fold_ref, peak_ref, mean_ref, square_ref, flip_ref = refs[2 * calls:]
    half, side = peak_ref.shape[1:]
    mid = side // 2
    pairs = [(keep, recv, n) for keep, recv in zip(keeps, recvs) for n in range(keep.shape[0])]
    count = len(pairs)
    for block in range(half // 8):
        rows = pl.ds(block * 8, 8)
        best = total = squares = None
        for keep, recv, n in pairs:
            power = (keep[n, half:half + 8] + recv[n, half:half + 8]) * (1.0 / entries)
            scale = lax.rsqrt(power + 1e-6) * (1.0 / side)
            c = (keep[n, rows] + recv[n, rows]) * scale
            if best is None:
                best, total, squares = c, c, c * c
            else:
                best, total, squares = jnp.maximum(best, c), total + c, squares + c * c
        total = total * (1.0 / count)
        squares = squares * (1.0 / count)
        for n, (ref, value) in enumerate(((peak_ref, best), (mean_ref, total), (square_ref, squares))):
            ref[0, rows, :mid] = value[:, :mid]
            flip_ref[pl.ds(n * half + block * 8, 8)] = value[:, mid:]
    right = jnp.dot(flip_ref[...], fold_ref[...], precision=lax.Precision.HIGHEST, preferred_element_type=jnp.float32)
    for n, ref in enumerate((peak_ref, mean_ref, square_ref)):
        ref[0, :, mid:] = right[n * half:(n + 1) * half]


def flipped(x, axis, bits):
    return lax.ppermute(x, axis, [(i, i ^ bits) for i in range(lax.axis_size(axis))])


def shards(spectra, templates, weights):
    half, side = spectra.shape[2:]
    orients = lax.axis_size("orient")
    vmem = pl.BlockSpec(memory_space=pltpu.VMEM)
    hbm = pl.BlockSpec(memory_space=pltpu.HBM)
    params = pltpu.CompilerParams(vmem_limit_bytes=24 << 20)
    shape = lambda *dims, dtype=jnp.float32: jax.ShapeDtypeStruct(dims, dtype)
    scratch = lambda *dims: pltpu.VMEM(dims, jnp.float32)
    template = templates[0]

    coef, table, columns = pl.pallas_call(
        prepare_kernel,
        in_specs=[hbm] * 3,
        out_specs=[vmem] * 3,
        out_shape=[shape(4, half, side)] + [shape(2, side, side, dtype=jnp.bfloat16)] * 2,
        scratch_shapes=[
            scratch(2, half, side), scratch(half, side), scratch(side, side), scratch(side, side), pltpu.SemaphoreType.DMA((5,)),
        ],
        compiler_params=params,
        name="prepare",
    )(spectra[0], weights, jnp.asarray(np.stack([row_table(side, half), column_table(side)])))

    def maps(wholes, arrays=(), places=(), extra=8):
        return pl.pallas_call(
            functools.partial(maps_kernel, len(wholes), places),
            in_specs=[vmem] * (3 + len(wholes) + len(arrays)),
            out_specs=[vmem] * 2,
            out_shape=[shape(len(wholes) + len(places), half + extra, side)] * 2,
            compiler_params=params,
            name="maps",
        )(coef, table, columns, *wholes, *arrays)

    if lax.axis_size("groups") == 2 and orients == 8:
        plane = lax.axis_index("groups")
        most = half - 8
        pick = lambda whole, n: lax.dynamic_index_in_dim(whole, n, 0, keepdims=False)
        part = pick(template, plane)
        near1, near2 = (flipped(part, "orient", 2 * k) for k in (1, 2))
        beside = flipped(lax.optimization_barrier((template, part))[0], "orient", 1)
        near1, near2, beside = lax.optimization_barrier((near1, near2, beside))
        near = jnp.concatenate([near1, near2], 0)
        far = flipped(jnp.concatenate([near2, pick(beside, 1 - plane)], 0), "orient", 2)
        near_x = flipped(near, "groups", 1)
        near_y = flipped(near, "orient", 1)
        far, near_x, near_y, coef = lax.optimization_barrier((far, near_x, near_y, coef))
        last_x = flipped(jnp.concatenate([far[:half], near_y[half:side - 8]], 0), "groups", 1)
        last_y = flipped(jnp.concatenate([far[:half], near_x[side - 8:]], 0), "orient", 1)
        corner = flipped(near_x[half:], "orient", 3)
        block = lambda array, start=0, rows=half: ((array, start, start + rows),)
        early = maps(
            [template, beside],
            [near, near_x, near_y, far],
            ((block(0), block(1)), (block(0, half), block(1, half)), (block(2), block(3, half))),
        )
        last_x, last_y, corner, early = lax.optimization_barrier((last_x, last_y, corner, early))
        late = maps(
            [],
            [near_y, last_x, last_y, far, corner],
            (
                (block(0, half), block(1, half, most) + block(2, half, 8)),
                (block(3), block(1)),
                (block(2), block(4)),
            ),
        )
        calls = [early, late]
    else:
        rest = [template] + [flipped(template, "orient", k) for k in range(1, orients)]
        calls = [maps(rest[i:i + 4]) for i in range(0, len(rest), 4)]
    keeps = [keep for keep, _ in calls]
    recvs = [flipped(send, "tile", 1) for _, send in calls]
    return tuple(pl.pallas_call(
        functools.partial(stats_kernel, len(keeps), 2 * side * side),
        in_specs=[vmem] * (2 * len(keeps) + 1),
        out_specs=[vmem] * 3,
        out_shape=[shape(1, half, side)] * 3,
        scratch_shapes=[scratch(3 * half, side // 2)],
        compiler_params=params,
        name="statistics",
    )(*keeps, *recvs, jnp.asarray(unfold_table(side // 2))))


def solution(mesh):
    in_specs = (
        P(("groups", "orient"), None, "tile", None),
        P("orient", None, "tile", None),
        P("groups", None),
    )
    out_specs = (P(("groups", "orient"), "tile", None),) * 3
    return jax.shard_map(shards, mesh=mesh, in_specs=in_specs, out_specs=out_specs, check_vma=False)
```

```python
import functools
import math

import jax
import jax.numpy as jnp
import numpy as np
from jax import lax
from jax.experimental import pallas as pl
from jax.experimental.pallas import tpu as pltpu
from jax.sharding import PartitionSpec as P


def column_table(side):
    mid = side // 2
    k = np.arange(side)[:, None]
    x = np.arange(mid)[None, :]
    angle = 2.0 * math.pi * (k * x % side) / side
    right = np.sin(angle)
    right[:, 0] = np.cos(math.pi * k[:, 0])
    return np.concatenate([np.cos(angle), right], 1).astype(np.float32)


def row_table(side, half):
    y = np.arange(side)[:, None]
    k = np.arange(half)[None, :]
    angle = 2.0 * math.pi * (k * y % side) / side
    return np.concatenate([np.cos(angle), -np.sin(angle)], 1).astype(np.float32)


def unfold_table(mid):
    table = np.zeros((mid, mid), np.float32)
    k = np.arange(mid)
    table[(mid - k) % mid, k] = 1.0
    return table


def parts(x):
    high = x.astype(jnp.bfloat16)
    low = (x - high.astype(jnp.float32)).astype(jnp.bfloat16)
    return high, low


def dot(a, b):
    return jnp.dot(a, b, preferred_element_type=jnp.float32)


def prepare_kernel(s_hbm, w_hbm, table_hbm, coef_ref, rt_ref, ct_ref, s_ref, w_ref, row_ref, col_ref, sems):
    half, side = w_ref.shape
    here = lax.axis_index("tile")
    swap = lax.axis_index("groups") % 2
    mine = pl.ds(pl.multiple_of(here * half, half), half)
    other = pl.ds(pl.multiple_of((1 - here) * half, half), half)
    moves = (
        (s_hbm, s_ref),
        (w_hbm.at[mine], w_ref),
        (table_hbm.at[0, mine], row_ref.at[pl.ds(0, half)]),
        (table_hbm.at[0, other], row_ref.at[pl.ds(half, half)]),
        (table_hbm.at[1], col_ref),
    )
    copies = [pltpu.make_async_copy(source, target, sems.at[n]) for n, (source, target) in enumerate(moves)]
    for copy in copies:
        copy.start()
    for copy in copies:
        copy.wait()
    w = w_ref[...]
    u, v = s_ref[swap] * w, s_ref[1 - swap] * w
    turn = (1 - 2 * swap).astype(jnp.float32)
    coef_ref[0], coef_ref[1], coef_ref[2], coef_ref[3] = u, v, u * turn, v * turn
    ct_ref[0], ct_ref[1] = parts(col_ref[...])
    odd = lax.broadcasted_iota(jnp.int32, (side, side), 0) % 2
    rt_ref[0], rt_ref[1] = parts(row_ref[...] * (1 - 2 * odd * here).astype(jnp.float32))


def correlate(a, b, coef_ref, col_ref, rt_ref, keep_ref, send_ref, n):
    half, side = a.shape
    mid = side // 2
    squares = jnp.sum((a * a + b * b).reshape(half // 8, 8, side), axis=0)
    power = jnp.broadcast_to(jnp.sum(squares), (keep_ref.shape[1] - half, side))
    z = jnp.concatenate([coef_ref[0] * a + coef_ref[1] * b, coef_ref[3] * a - coef_ref[2] * b], 0)
    zh, zl = parts(z)
    ch, cl = col_ref[0], col_ref[1]
    m = dot(zh, ch) + (dot(zl, ch) + dot(zh, cl))
    mcr, mci = m[:half, :mid], m[half:, :mid]
    msr, msi = m[:half, mid:], m[half:, mid:]
    first = lax.broadcasted_iota(jnp.int32, (half, mid), 1) == 0
    real = jnp.concatenate([mcr - jnp.where(first, 0.0, msi), jnp.where(first, msr, mcr + msi)], 1)
    imag = jnp.concatenate([mci + jnp.where(first, 0.0, msr), jnp.where(first, msi, mci - msr)], 1)
    ah, al = parts(jnp.concatenate([real, imag], 0))
    rh, rl = rt_ref[0], rt_ref[1]
    p = dot(rh, ah) + (dot(rh, al) + dot(rl, ah))
    keep_ref[n, :half] = p[:half]
    keep_ref[n, half:] = power
    send_ref[n, :half] = p[half:]
    send_ref[n, half:] = power


def maps_kernel(wholes, places, coef_ref, rt_ref, col_ref, *refs):
    inputs, (keep_ref, send_ref) = refs[:-2], refs[-2:]
    whole_refs, part_refs = inputs[:wholes], inputs[wholes:]
    swap = lax.axis_index("groups") % 2
    for n, ref in enumerate(whole_refs):
        correlate(ref[swap], ref[1 - swap], coef_ref, col_ref, rt_ref, keep_ref, send_ref, n)
    for n, pair in enumerate(places):
        a, b = (jnp.concatenate([part_refs[array][start:stop] for array, start, stop in pieces], 0) for pieces in pair)
        correlate(a, b, coef_ref, col_ref, rt_ref, keep_ref, send_ref, wholes + n)


def stats_kernel(calls, entries, *refs):
    keeps, recvs = refs[:calls], refs[calls:2 * calls]
    fold_ref, peak_ref, mean_ref, square_ref, flip_ref = refs[2 * calls:]
    half, side = peak_ref.shape[1:]
    mid = side // 2
    pairs = [(keep, recv, n) for keep, recv in zip(keeps, recvs) for n in range(keep.shape[0])]
    count = len(pairs)
    scales = []
    for keep, recv, n in pairs:
        power = (keep[n, half:half + 8] + recv[n, half:half + 8]) * (1.0 / entries)
        scales.append(lax.rsqrt(power + 1e-6) * (1.0 / side))
    for block in range(half // 8):
        rows = pl.ds(block * 8, 8)
        best = total = squares = None
        for (keep, recv, n), scale in zip(pairs, scales):
            c = (keep[n, rows] + recv[n, rows]) * scale
            if best is None:
                best, total, squares = c, c, c * c
            else:
                best, total, squares = jnp.maximum(best, c), total + c, squares + c * c
        total = total * (1.0 / count)
        squares = squares * (1.0 / count)
        for n, (ref, value) in enumerate(((peak_ref, best), (mean_ref, total), (square_ref, squares))):
            ref[0, rows, :mid] = value[:, :mid]
            flip_ref[pl.ds(n * half + block * 8, 8)] = value[:, mid:]
    right = jnp.dot(flip_ref[...], fold_ref[...], precision=lax.Precision.HIGHEST, preferred_element_type=jnp.float32)
    for n, ref in enumerate((peak_ref, mean_ref, square_ref)):
        ref[0, :, mid:] = right[n * half:(n + 1) * half]


def flipped(x, axis, bits):
    return lax.ppermute(x, axis, [(i, i ^ bits) for i in range(lax.axis_size(axis))])


def shards(spectra, templates, weights):
    half, side = spectra.shape[2:]
    orients = lax.axis_size("orient")
    vmem = pl.BlockSpec(memory_space=pltpu.VMEM)
    hbm = pl.BlockSpec(memory_space=pltpu.HBM)
    params = pltpu.CompilerParams(vmem_limit_bytes=24 << 20)
    shape = lambda *dims, dtype=jnp.float32: jax.ShapeDtypeStruct(dims, dtype)
    scratch = lambda *dims: pltpu.VMEM(dims, jnp.float32)
    template = templates[0]

    coef, table, columns = pl.pallas_call(
        prepare_kernel,
        in_specs=[hbm] * 3,
        out_specs=[vmem] * 3,
        out_shape=[shape(4, half, side)] + [shape(2, side, side, dtype=jnp.bfloat16)] * 2,
        scratch_shapes=[
            scratch(2, half, side), scratch(half, side), scratch(side, side), scratch(side, side), pltpu.SemaphoreType.DMA((5,)),
        ],
        compiler_params=params,
        name="prepare",
    )(spectra[0], weights, jnp.asarray(np.stack([row_table(side, half), column_table(side)])))

    def maps(wholes, arrays=(), places=(), extra=8):
        return pl.pallas_call(
            functools.partial(maps_kernel, len(wholes), places),
            in_specs=[vmem] * (3 + len(wholes) + len(arrays)),
            out_specs=[vmem] * 2,
            out_shape=[shape(len(wholes) + len(places), half + extra, side)] * 2,
            compiler_params=params,
            name="maps",
        )(coef, table, columns, *wholes, *arrays)

    if lax.axis_size("groups") == 2 and orients == 8:
        plane = lax.axis_index("groups")
        most = half - 8
        pick = lambda whole, n: lax.dynamic_index_in_dim(whole, n, 0, keepdims=False)
        part = pick(template, plane)
        near1, near2 = (flipped(part, "orient", 2 * k) for k in (1, 2))
        beside = flipped(lax.optimization_barrier((template, part))[0], "orient", 1)
        near1, near2, beside = lax.optimization_barrier((near1, near2, beside))
        near = jnp.concatenate([near1, near2], 0)
        far = flipped(jnp.concatenate([near2, pick(beside, 1 - plane)], 0), "orient", 2)
        near_x = flipped(near, "groups", 1)
        near_y = flipped(near, "orient", 1)
        far, near_x, near_y, coef = lax.optimization_barrier((far, near_x, near_y, coef))
        last_x = flipped(jnp.concatenate([far[:half], near_y[half:side - 8]], 0), "groups", 1)
        last_y = flipped(jnp.concatenate([far[:half], near_x[side - 8:]], 0), "orient", 1)
        corner = flipped(near_x[half:], "orient", 3)
        block = lambda array, start=0, rows=half: ((array, start, start + rows),)
        early = maps(
            [template, beside],
            [near, near_x, near_y, far],
            ((block(0), block(1)), (block(0, half), block(1, half)), (block(2), block(3, half))),
        )
        last_x, last_y, corner, early = lax.optimization_barrier((last_x, last_y, corner, early))
        late = maps(
            [],
            [near_y, last_x, last_y, far, corner],
            (
                (block(0, half), block(1, half, most) + block(2, half, 8)),
                (block(3), block(1)),
                (block(2), block(4)),
            ),
        )
        calls = [early, late]
    else:
        rest = [template] + [flipped(template, "orient", k) for k in range(1, orients)]
        calls = [maps(rest[i:i + 4]) for i in range(0, len(rest), 4)]
    keeps = [keep for keep, _ in calls]
    recvs = [flipped(send, "tile", 1) for _, send in calls]
    return tuple(pl.pallas_call(
        functools.partial(stats_kernel, len(keeps), 2 * side * side),
        in_specs=[vmem] * (2 * len(keeps) + 1),
        out_specs=[vmem] * 3,
        out_shape=[shape(1, half, side)] * 3,
        scratch_shapes=[scratch(3 * half, side // 2)],
        compiler_params=params,
        name="statistics",
    )(*keeps, *recvs, jnp.asarray(unfold_table(side // 2))))


def solution(mesh):
    in_specs = (
        P(("groups", "orient"), None, "tile", None),
        P("orient", None, "tile", None),
        P("groups", None),
    )
    out_specs = (P(("groups", "orient"), "tile", None),) * 3
    return jax.shard_map(shards, mesh=mesh, in_specs=in_specs, out_specs=out_specs, check_vma=False)
```
